512 devices in a mesh: pair: 128 (over z, x, y_lo, core), dp: 4 (over y_hi).
Axes of the slice: x: 4, y: 8 (y_hi: 4, y_lo: 2; y = y_hi * 2 + y_lo), z: 8, core: 2. Of those that a mesh axis runs over, the one named last changes fastest.
Arguments:
- encoder_activations: bfloat16 [131072, 1024], P(('pair', 'dp')), may hold values from -0.75 to 0.75
- mapping_matrix: bfloat16 [1024, 1024], replicated, may hold values from -0.1875 to 0.1875
- affinity_sharpness: float32 [1], replicated, may hold values from 4 to 8
- affinity_offset: float32 [1], replicated, may hold values from -3 to -1
- segment_number_at_slot: int32 [128], replicated, may hold values from 0 to 127, as said below
- positive_match_targets: int32 [131072], P(('pair', 'dp')), may hold values from 0 to 32767, as said below
Outputs:
- grad_features: bfloat16 [131072, 1024], P(('pair', 'dp'))
- grad_proj: float32 [1024, 1024], P('pair')
The draws below stay inside these ranges and needn't reach their ends.
Inputs may be any that keep to these rules, and one draw needn't show every extreme that they name: `segment_number_at_slot`: a permutation of the block numbers, the same for every dp index. `positive_match_targets`: the block-row index of the row's positive within its dp group; the relation is mutual and no row is its own positive.
All inputs are finite; a program needn't handle non-finite values.
Results may differ from the reference program's by a relative error of at most 0.0056.
Values may be sent and summed in bfloat16 or wider, within the bound.
A program may use at most 64 MiB of HBM per device.

```python
import jax
import jax.numpy as jnp
from jax import lax

D = 1024
B_DEV = 256
ROUNDS = 2
BLOCKS = 128
GROUP_COPIES = 4
GROUP_ROWS = 32768
ROWS = 131072


def seating(key):
    return jax.random.permutation(key, BLOCKS).astype(jnp.int32)


def draw_segment_number_at_slot(key, part):
    seats = seating(key)
    return seats


def draw_positive_match_targets(key, part):
    seats = seating(key)
    key = jax.random.fold_in(key, 12)

    def mates_for(group_key):
        order = jax.random.permutation(group_key, GROUP_ROWS).astype(jnp.int32)
        firsts = order[0::2]
        seconds = order[1::2]
        mates = jnp.zeros((GROUP_ROWS,), jnp.int32)
        return mates.at[firsts].set(seconds).at[seconds].set(firsts)
    group_keys = jax.random.split(key, GROUP_COPIES)
    mates = jax.vmap(mates_for)(group_keys)
    block_gid = seats[:, None] * B_DEV + jnp.arange(B_DEV, dtype=jnp.int32)[None, :]
    chosen = mates[:, block_gid]
    return jnp.transpose(chosen, (1, 0, 2)).reshape(ROWS).astype(jnp.int32)


def strengthened(drawn, stream_key, source, target, shards_of, factor):
    owner, partner = [(jnp.arange(drawn.shape[dim]) // (drawn.shape[dim] // shards_of)).reshape([-1 if axis == dim else 1 for axis in range(drawn.ndim)]) for dim in (source, target)]
    chosen = jax.random.permutation(stream_key, shards_of)[partner]
    strong = (owner == chosen) | (owner == (partner + shards_of // 2) % shards_of)
    return jnp.where(strong, factor * drawn, drawn)


def block_scale(own_key, shape, shards, low, top_value):
    loudness, own = 1.0, jax.random.fold_in(own_key, 6)
    for axis_at, parts in shards:
        heights = jnp.exp(jax.random.uniform(jax.random.fold_in(own, axis_at), (parts,), jnp.float32, low / len(shards), top_value / len(shards)))
        loudness = loudness * jnp.repeat(heights, shape[axis_at] // parts).reshape([-1 if axis == axis_at else 1 for axis in range(len(shape))])
    return loudness


def noise(rng, extent, spread, limit, shards=(), held_as=jnp.bfloat16):
    result = spread * jax.random.normal(rng, extent, jnp.float32)
    if shards:
        result = result * block_scale(rng, extent, shards, -0.22, 0.18)
    return jnp.clip(result, -limit, limit).astype(held_as)


def bell_draw_with(key, extent, deviation, reach, cuts, heavy, held_as=jnp.bfloat16):
    array = deviation * jax.random.normal(key, extent, jnp.float32)
    if cuts:
        array = array * block_scale(key, extent, cuts, -0.22, 0.18)
    return jnp.clip(strengthened(array, jax.random.fold_in(key, 3), *heavy), -reach, reach).astype(held_as)


def setup_inputs(seed: int = 0) -> dict:
    seeds = jax.random.split(jax.random.key(seed), 7)
    return {
        "encoder_activations": bell_draw_with(seeds[0], (ROWS, D), 0.03125, 0.75, ((0, 512),), (0, 1, 512, 6.0)),
        "mapping_matrix": noise(seeds[1], (D, D), D ** -0.5, 0.1875),
        "affinity_sharpness": jnp.clip(jax.random.uniform(seeds[2], (1,), jnp.float32, 4.0, 8.0), 4.0, 8.0),
        "affinity_offset": jnp.clip(jax.random.uniform(seeds[3], (1,), jnp.float32, -3.0, -1.0), -3.0, -1.0),
        "segment_number_at_slot": draw_segment_number_at_slot(jax.random.fold_in(seeds[6], 71), 0),
        "positive_match_targets": draw_positive_match_targets(jax.random.fold_in(seeds[6], 71), 0),
    }


epsilon = 1e-06

def embed(row_block, weight):
    projected = jnp.dot(row_block, weight, preferred_element_type=jnp.float32)
    inverse_norm = lax.rsqrt(lax.optimization_barrier(jnp.sum(projected * projected, axis=-1, keepdims=True)) + epsilon)
    return (projected, inverse_norm, (projected * inverse_norm).astype(jnp.bfloat16))

def pair_weights_lookup(local_rows, other_rows, other_group_index, local_labels, smoothing_factor, shift_amount, group_copies, identical_block):
    pair_logits = lax.dot_general(local_rows, other_rows, (((1,), (1,)), ((), ())), preferred_element_type=jnp.float32)
    pair_logits = pair_logits * smoothing_factor + shift_amount
    signs = jnp.where(local_labels[:, None] == other_group_index[None, :], 1.0, -1.0).astype(jnp.float32)
    pair_coefficient = -signs * jax.nn.sigmoid(-signs * pair_logits) / group_copies
    if identical_block:
        row_ids = lax.broadcasted_iota(jnp.int32, pair_coefficient.shape, 0)
        col_ids = lax.broadcasted_iota(jnp.int32, pair_coefficient.shape, 1)
        pair_coefficient = jnp.where(row_ids == col_ids, jnp.zeros_like(pair_coefficient), pair_coefficient)
    pairing_weight = (2.0 * smoothing_factor * pair_coefficient).astype(jnp.bfloat16)
    return jnp.dot(pairing_weight, other_rows, preferred_element_type=jnp.float32)

def reference(encoder_activations, mapping_matrix, affinity_sharpness, affinity_offset, segment_number_at_slot, positive_match_targets):
    grouped = encoder_activations.reshape(BLOCKS, GROUP_COPIES, B_DEV, D)
    grouped_labels = positive_match_targets.reshape(BLOCKS, GROUP_COPIES, B_DEV)
    smoothing_factor = affinity_sharpness[0]
    shift_amount = affinity_offset[0]

    def embed_block(block_rows):
        return embed(block_rows.reshape(GROUP_COPIES * B_DEV, D), mapping_matrix)[2].reshape(GROUP_COPIES, B_DEV, D)
    all_embedded = lax.map(embed_block, grouped)
    row_local = jnp.arange(B_DEV, dtype=jnp.int32)

    def step(running, block_index):
        own_rows = grouped[block_index].reshape(GROUP_COPIES * B_DEV, D)
        projected, inverse_norm, embedded_rows = embed(own_rows, mapping_matrix)
        embedded_rows = embedded_rows.reshape(GROUP_COPIES, B_DEV, D)
        own_labels = grouped_labels[block_index]
        own_group_index = segment_number_at_slot[block_index] * B_DEV + row_local

        def self_tile(local_rows, local_labels):
            return pair_weights_lookup(local_rows, local_rows, own_group_index, local_labels, smoothing_factor, shift_amount, GROUP_COPIES, True)
        grad_embedded = jax.vmap(self_tile)(embedded_rows, own_labels)
        for round_bit in range(ROUNDS):
            partner = jnp.bitwise_xor(block_index, 1 << round_bit).astype(jnp.int32)
            theirs_all = all_embedded[partner]
            partner_group_index = segment_number_at_slot[partner] * B_DEV + row_local

            def cross_tile(local_rows, other_rows, local_labels):
                return pair_weights_lookup(local_rows, other_rows, partner_group_index, local_labels, smoothing_factor, shift_amount, GROUP_COPIES, False)
            grad_embedded = grad_embedded + jax.vmap(cross_tile)(embedded_rows, theirs_all, own_labels)
        grad_embedded = grad_embedded.reshape(GROUP_COPIES * B_DEV, D)
        inner = lax.optimization_barrier(jnp.sum(projected * grad_embedded, axis=-1, keepdims=True))
        grad_pre = (inverse_norm * grad_embedded - inverse_norm ** 3 * inner * projected).astype(jnp.bfloat16)
        grad_rows = lax.dot_general(grad_pre, mapping_matrix, (((1,), (1,)), ((), ())), preferred_element_type=jnp.float32).astype(jnp.bfloat16)
        running = running + lax.dot_general(own_rows, grad_pre, (((0,), (0,)), ((), ())), preferred_element_type=jnp.float32)
        return (running, grad_rows)
    grad_proj, grad_blocks = lax.scan(step, jnp.zeros((D, D), jnp.float32), jnp.arange(BLOCKS, dtype=jnp.int32))
    return (grad_blocks.reshape(ROWS, D), grad_proj)
```

```python
import functools

import jax
import jax.numpy as jnp
from jax import lax
from jax.experimental import pallas as pl
from jax.experimental.pallas import tpu as pltpu
from jax.sharding import PartitionSpec as P

EPSILON = 1e-06
NX = 4
CHUNKS = 2
F32 = jnp.float32
BF16 = jnp.bfloat16


def dot_nn(a, b):
    return jnp.dot(a, b, preferred_element_type=F32)


def dot_nt(a, b):
    return lax.dot_general(a, b, (((1,), (1,)), ((), ())), preferred_element_type=F32)


def dot_tn(a, b):
    return lax.dot_general(a, b, (((0,), (0,)), ((), ())), preferred_element_type=F32)


def kernel(
    nz,
    nx,
    groups,
    sharp_ref,
    offset_ref,
    seg_ref,
    lab_hbm,
    feat_hbm,
    map_hbm,
    gf_hbm,
    gp_ref,
    feats,
    labels,
    mapping,
    proj,
    inv,
    emb,
    grad_emb,
    grad_pre,
    turned,
    lhs,
    partial,
    mine,
    core_out,
    core_in,
    x_out,
    x_in,
    z_out,
    z_in,
    y_in,
    gf_vmem,
    local_sem,
    feat_sem,
    emb_sem,
    core_sem,
    x_sem,
    z_sem,
    y_sem,
):
    rows, width = feat_hbm.shape
    half = width // 2
    step = rows // CHUNKS
    pair = lax.axis_index("pair")
    group = lax.axis_index("dp")
    core = pair % 2
    y_lo = (pair // 2) % 2
    x_at = (pair // 4) % nx
    z_at = pair // (4 * nx)
    core_mate = pair + 1 - 2 * core
    y_mate = pair + 2 - 4 * y_lo
    diag_mate = y_mate + 1 - 2 * core
    x_mates = [pair + ((x_at + d) % nx - x_at) * 4 for d in range(1, nx)]
    z_mates = [pair + ((z_at + d) % nz - z_at) * (4 * nx) for d in range(1, nz)]
    y_groups = [(group + d) % groups for d in range(1, groups)]
    to_core, to_y = {"pair": core_mate}, {"pair": y_mate}

    load_feat = pltpu.make_async_copy(feat_hbm, feats.at[0], local_sem.at[0])
    load_map = pltpu.make_async_copy(map_hbm, mapping, local_sem.at[1])
    load_lab = pltpu.make_async_copy(lab_hbm, labels.at[0], local_sem.at[2])
    load_feat.start()
    load_map.start()
    load_lab.start()

    def remote(src, dst, sems, at, device):
        return pltpu.make_async_remote_copy(
            src_ref=src,
            dst_ref=dst,
            send_sem=sems.at[0, at],
            recv_sem=sems.at[1, at],
            device_id=device,
            device_id_type=pl.DeviceIdType.MESH,
        )

    barrier = pltpu.get_barrier_semaphore()
    greeted = [to_core, to_y]
    greeted += [{"pair": mate} for mate in x_mates + z_mates]
    greeted += [{"dp": other} for other in y_groups]
    for device in greeted:
        pl.semaphore_signal(barrier, inc=1, device_id=device, device_id_type=pl.DeviceIdType.MESH)
    pl.semaphore_wait(barrier, len(greeted))

    send_feat = []
    for j in range(CHUNKS):
        part = pl.ds(j * step, step)
        send_feat.append(remote(feat_hbm.at[part], feats.at[1, part], feat_sem, j, to_y))
        send_feat[-1].start()
    send_lab = remote(lab_hbm, labels.at[1], feat_sem, CHUNKS, to_y)
    send_lab.start()

    sharp = sharp_ref[0]
    offset = offset_ref[0]

    def embed(slot, part):
        projected = dot_nn(feats[slot, part], mapping[...])
        norm = lax.rsqrt(jnp.sum(projected * projected, axis=-1, keepdims=True) + EPSILON)
        proj[slot, part] = projected
        inv[slot, part] = norm
        emb[slot, part] = (projected * norm).astype(BF16)

    def turn(slot, part, at):
        flipped = feats[slot, part].T.reshape(turned.shape[:4] + (part.size,))
        turned[:, :, :, :, pl.ds(at, part.size)] = flipped

    def weights(left, right, left_first, right_labels, same):
        logits = dot_nt(left, right) * sharp + offset
        row = lax.broadcasted_iota(jnp.int32, logits.shape, 0)
        hit = jnp.where(right_labels == row + left_first, 1.0, 0.0)
        weight = (2.0 / groups * sharp) * (jax.nn.sigmoid(logits) - hit)
        if same:
            column = lax.broadcasted_iota(jnp.int32, logits.shape, 1)
            weight = jnp.where(row == column, 0.0, weight)
        return weight.astype(BF16)

    whole = pl.ds(0, rows)

    load_feat.wait()
    load_map.wait()
    load_lab.wait()
    embed(0, whole)
    send_own = remote(emb.at[0], emb.at[2], emb_sem, 0, to_core)
    send_own.start()
    turn(0, whole, 0)

    own = emb[0]
    weight = weights(own, own, seg_ref[pair] * rows, labels[0], True)
    grad_emb[0] = dot_nn(weight, own)
    send_own.wait_recv()
    weight = weights(emb[2], own, seg_ref[core_mate] * rows, labels[0], False)
    grad_emb[0] += dot_tn(weight, emb[2])

    send_theirs = []
    for j in range(CHUNKS):
        part = pl.ds(j * step, step)
        send_feat[j].wait_recv()
        embed(1, part)
        send_theirs.append(remote(emb.at[1, part], emb.at[3, part], emb_sem, 1 + j, to_core))
        send_theirs[-1].start()
        weight = weights(
            emb[1, part], emb[0], seg_ref[y_mate] * rows + j * step, labels[0], False
        )
        grad_emb[0] += dot_tn(weight, emb[1, part])
        grad_emb[1, part] = dot_nn(weight, emb[0])
        turn(1, part, rows + j * step)

    def finish(slot):
        grad = grad_emb[slot]
        projected = proj[slot]
        norm = inv[slot]
        inner = jnp.sum(projected * grad, axis=-1, keepdims=True)
        grad_pre[pl.ds(slot * rows, rows)] = (
            norm * grad - norm**3 * inner * projected
        ).astype(BF16)

    send_lab.wait_recv()
    finish(0)
    theirs = emb[1]
    weight = weights(theirs, theirs, seg_ref[y_mate] * rows, labels[1], True)
    grad_emb[1] += dot_nn(weight, theirs)
    for x in range(nx):
        lhs[x] = turned[:, x, y_lo]
    for copy in send_theirs:
        copy.wait_recv()
    weight = weights(emb[3], emb[1], seg_ref[diag_mate] * rows, labels[1], False)
    grad_emb[1] += dot_tn(weight, emb[3])
    finish(1)

    product = dot_nn(lhs[...].reshape(nx * nz * 16, 2 * rows), grad_pre[...])
    partial[...] = product.reshape(nx, nz, 2, 8, width)

    def stacked(block):
        return jnp.concatenate([block[..., :half], block[..., half:]], axis=-2)

    core_out[...] = stacked(partial[:, :, 1 - core]).astype(BF16)
    send_core = remote(core_out, core_in, core_sem, 0, to_core)
    send_core.start()
    mine[...] = stacked(partial[:, :, core])
    send_core.wait_recv()
    total = mine[...] + core_in[...].astype(F32)
    mine[...] = total
    x_out[...] = total.astype(BF16)
    send_x = []
    for d in range(1, nx):
        copy = remote(
            x_out.at[(x_at + d) % nx], x_in.at[d - 1], x_sem, d - 1, {"pair": x_mates[d - 1]}
        )
        copy.start()
        send_x.append(copy)

    gf_vmem[...] = dot_nt(grad_pre[pl.ds(0, rows)], mapping[...]).astype(BF16)
    store_gf = pltpu.make_async_copy(gf_vmem, gf_hbm, local_sem.at[3])
    store_gf.start()

    total = mine[x_at]
    for d in range(1, nx):
        send_x[d - 1].wait_recv()
        total = total + x_in[d - 1].astype(F32)
    mine[0] = total
    z_out[...] = total.astype(BF16)
    send_z = []
    for d in range(1, nz):
        copy = remote(
            z_out.at[(z_at + d) % nz], z_in.at[d - 1], z_sem, d - 1, {"pair": z_mates[d - 1]}
        )
        copy.start()
        send_z.append(copy)
    total = mine[0, z_at]
    for d in range(1, nz):
        send_z[d - 1].wait_recv()
        total = total + z_in[d - 1].astype(F32)
    y_in[group] = total.astype(BF16)
    send_y = []
    for d in range(1, groups):
        copy = remote(y_in.at[group], y_in.at[group], y_sem, d - 1, {"dp": y_groups[d - 1]})
        copy.start()
        send_y.append(copy)
    for copy in send_y:
        copy.wait_recv()
    total = y_in[0].astype(F32)
    for at in range(1, groups):
        total = total + y_in[at].astype(F32)
    gp_ref[...] = jnp.concatenate([total[:8], total[8:]], axis=-1)

    store_gf.wait()
    sent = send_feat + [send_lab, send_own] + send_theirs + [send_core] + send_x + send_z + send_y
    for copy in sent:
        copy.wait_send()


def body(nz, nx, groups, feats, mapping, sharp, offset, segments, targets):
    rows, width = feats.shape
    half = width // 2
    smem = pl.BlockSpec(memory_space=pltpu.SMEM)
    anywhere = pl.BlockSpec(memory_space=pl.ANY)

    def sems(n):
        return pltpu.SemaphoreType.DMA((2, n))

    return pl.pallas_call(
        functools.partial(kernel, nz, nx, groups),
        out_shape=(
            jax.ShapeDtypeStruct((rows, width), BF16),
            jax.ShapeDtypeStruct((8, width), F32),
        ),
        in_specs=[smem, smem, smem, anywhere, anywhere, anywhere],
        out_specs=(anywhere, pl.BlockSpec(memory_space=pltpu.VMEM)),
        scratch_shapes=[
            pltpu.VMEM((2, rows, width), BF16),
            pltpu.VMEM((2, 1, rows), jnp.int32),
            pltpu.VMEM((width, width), BF16),
            pltpu.VMEM((2, rows, width), F32),
            pltpu.VMEM((2, rows, 1), F32),
            pltpu.VMEM((4, rows, width), BF16),
            pltpu.VMEM((2, rows, width), F32),
            pltpu.VMEM((2 * rows, width), BF16),
            pltpu.VMEM((nz, nx, 2, 16, 2 * rows), BF16),
            pltpu.VMEM((nx, nz, 16, 2 * rows), BF16),
            pltpu.VMEM((nx, nz, 2, 8, width), F32),
            pltpu.VMEM((nx, nz, 16, half), F32),
            pltpu.VMEM((nx, nz, 16, half), BF16),
            pltpu.VMEM((nx, nz, 16, half), BF16),
            pltpu.VMEM((nx, nz, 16, half), BF16),
            pltpu.VMEM((nx - 1, nz, 16, half), BF16),
            pltpu.VMEM((nz, 16, half), BF16),
            pltpu.VMEM((nz - 1, 16, half), BF16),
            pltpu.VMEM((groups, 16, half), BF16),
            pltpu.VMEM((rows, width), BF16),
            pltpu.SemaphoreType.DMA((4,)),
            sems(CHUNKS + 1),
            sems(CHUNKS + 1),
            sems(1),
            sems(nx - 1),
            sems(nz - 1),
            sems(groups - 1),
        ],
        compiler_params=pltpu.CompilerParams(
            collective_id=0, has_side_effects=True, vmem_limit_bytes=52 * 1024 * 1024
        ),
        cost_estimate=pl.CostEstimate(
            flops=2 * rows * width * (5 * width + 11 * rows),
            bytes_accessed=8 * rows * width,
            transcendentals=5 * rows * rows,
        ),
        name="contrastive",
    )(sharp, offset, segments, targets.reshape(1, rows), feats, mapping)


def solution(mesh, nx=NX):
    nz = mesh.shape["pair"] // (4 * nx)
    in_specs = (P(("pair", "dp"), None), P(), P(), P(), P(), P(("pair", "dp")))
    out_specs = (P(("pair", "dp"), None), P("pair", None))
    return jax.shard_map(
        functools.partial(body, nz, nx, mesh.shape["dp"]),
        mesh=mesh,
        in_specs=in_specs,
        out_specs=out_specs,
        check_vma=False,
    )
```

```python
import functools

import jax
import jax.numpy as jnp
from jax import lax
from jax.experimental import pallas as pl
from jax.experimental.pallas import tpu as pltpu
from jax.sharding import PartitionSpec as P

EPSILON = 1e-06
NX = 4
CHUNKS = 2
F32 = jnp.float32
BF16 = jnp.bfloat16


def dot_nn(a, b):
    return jnp.dot(a, b, preferred_element_type=F32)


def dot_nt(a, b):
    return lax.dot_general(a, b, (((1,), (1,)), ((), ())), preferred_element_type=F32)


def dot_tn(a, b):
    return lax.dot_general(a, b, (((0,), (0,)), ((), ())), preferred_element_type=F32)


def kernel(
    nz,
    nx,
    groups,
    sharp_ref,
    offset_ref,
    seg_hbm,
    lab_hbm,
    feat_hbm,
    map_hbm,
    gf_hbm,
    gp_ref,
    seg_ref,
    feats,
    labels,
    mapping,
    proj,
    inv,
    emb,
    grad_emb,
    grad_pre,
    turned,
    lhs,
    partial,
    mine,
    core_out,
    core_in,
    x_out,
    x_in,
    relay_out,
    z_sum,
    z_out,
    z_in,
    y_in,
    gf_vmem,
    local_sem,
    feat_sem,
    emb_sem,
    core_sem,
    x_sem,
    z_sem,
    y_sem,
):
    rows, width = feat_hbm.shape
    half, quarter = width // 2, width // 4
    step = rows // CHUNKS
    pair = lax.axis_index("pair")
    group = lax.axis_index("dp")
    core = pair % 2
    y_lo = (pair // 2) % 2
    x_at = (pair // 4) % nx
    z_at = pair // (4 * nx)
    core_mate = pair + 1 - 2 * core
    y_mate = pair + 2 - 4 * y_lo
    diag_mate = y_mate + 1 - 2 * core
    x_right, x_left, x_far = (x_at + 1) % nx, (x_at + nx - 1) % nx, (x_at + 2) % nx
    right, left = pair + (x_right - x_at) * 4, pair + (x_left - x_at) * 4
    z_mates = [pair + ((z_at + d) % nz - z_at) * (4 * nx) for d in range(1, nz)]
    y_groups = [(group + d) % groups for d in range(1, groups)]
    to_core, to_y = {"pair": core_mate}, {"pair": y_mate}

    load_feat = pltpu.make_async_copy(feat_hbm, feats.at[0], local_sem.at[0])
    load_map = pltpu.make_async_copy(map_hbm, mapping, local_sem.at[1])
    load_lab = pltpu.make_async_copy(lab_hbm, labels.at[0], local_sem.at[2])
    load_seg = pltpu.make_async_copy(seg_hbm, seg_ref, local_sem.at[4])
    loads = [load_feat, load_map, load_lab, load_seg]
    for copy in loads:
        copy.start()

    def remote(src, dst, sems, at, device):
        return pltpu.make_async_remote_copy(
            src_ref=src,
            dst_ref=dst,
            send_sem=sems.at[0, at],
            recv_sem=sems.at[1, at],
            device_id=device,
            device_id_type=pl.DeviceIdType.MESH,
        )

    barrier = pltpu.get_barrier_semaphore()
    greeted = [to_core, to_y]
    greeted += [{"pair": mate} for mate in [right, left] + z_mates]
    greeted += [{"dp": other} for other in y_groups]
    for device in greeted:
        pl.semaphore_signal(barrier, inc=1, device_id=device, device_id_type=pl.DeviceIdType.MESH)
    pl.semaphore_wait(barrier, len(greeted))

    send_feat = []
    for j in range(CHUNKS):
        part = pl.ds(j * step, step)
        send_feat.append(remote(feat_hbm.at[part], feats.at[1, part], feat_sem, j, to_y))
        send_feat[-1].start()
    send_lab = remote(lab_hbm, labels.at[1], feat_sem, CHUNKS, to_y)
    send_lab.start()

    def embed(slot, part):
        projected = dot_nn(feats[slot, part], mapping[...])
        norm = lax.rsqrt(jnp.sum(projected * projected, axis=-1, keepdims=True) + EPSILON)
        proj[slot, part] = projected
        inv[slot, part] = norm
        emb[slot, part] = (projected * norm).astype(BF16)

    def turn(slot, part, at):
        flipped = feats[slot, part].T.reshape(turned.shape[:4] + (part.size,))
        turned[:, :, :, :, pl.ds(at, part.size)] = flipped

    def weights(left, right, left_first, right_labels, same):
        logits = dot_nt(left, right) * sharp + offset
        row = lax.broadcasted_iota(jnp.int32, logits.shape, 0)
        hit = jnp.where(right_labels == row + left_first, 1.0, 0.0)
        weight = (2.0 / groups * sharp) * (jax.nn.sigmoid(logits) - hit)
        if same:
            column = lax.broadcasted_iota(jnp.int32, logits.shape, 1)
            weight = jnp.where(row == column, 0.0, weight)
        return weight.astype(BF16)

    whole = pl.ds(0, rows)

    load_feat.wait()
    load_map.wait()
    embed(0, whole)
    send_own = remote(emb.at[0], emb.at[2], emb_sem, 0, to_core)
    send_own.start()
    turn(0, whole, 0)

    for copy in loads[2:]:
        copy.wait()
    sharp = sharp_ref[0]
    offset = offset_ref[0]

    own = emb[0]
    weight = weights(own, own, seg_ref[pair] * rows, labels[0], True)
    grad_emb[0] = dot_nn(weight, own)
    send_own.wait_recv()
    weight = weights(emb[2], own, seg_ref[core_mate] * rows, labels[0], False)
    grad_emb[0] += dot_tn(weight, emb[2])

    send_theirs = []
    for j in range(CHUNKS):
        part = pl.ds(j * step, step)
        send_feat[j].wait_recv()
        embed(1, part)
        send_theirs.append(remote(emb.at[1, part], emb.at[3, part], emb_sem, 1 + j, to_core))
        send_theirs[-1].start()
        weight = weights(
            emb[1, part], emb[0], seg_ref[y_mate] * rows + j * step, labels[0], False
        )
        grad_emb[0] += dot_tn(weight, emb[1, part])
        grad_emb[1, part] = dot_nn(weight, emb[0])
        turn(1, part, rows + j * step)

    def finish(slot):
        grad = grad_emb[slot]
        projected = proj[slot]
        norm = inv[slot]
        inner = jnp.sum(projected * grad, axis=-1, keepdims=True)
        grad_pre[pl.ds(slot * rows, rows)] = (
            norm * grad - norm**3 * inner * projected
        ).astype(BF16)

    send_lab.wait_recv()
    finish(0)
    theirs = emb[1]
    weight = weights(theirs, theirs, seg_ref[y_mate] * rows, labels[1], True)
    grad_emb[1] += dot_nn(weight, theirs)
    for x in range(nx):
        lhs[x] = turned[:, x, y_lo]
    for copy in send_theirs:
        copy.wait_recv()
    weight = weights(emb[3], emb[1], seg_ref[diag_mate] * rows, labels[1], False)
    grad_emb[1] += dot_tn(weight, emb[3])
    finish(1)

    def stacked(block):
        return jnp.concatenate([block[..., :quarter], block[..., quarter:]], axis=-2)

    sent = []

    def send(src, dst, sems, at, device):
        copy = remote(src, dst, sems, at, device)
        copy.start()
        sent.append(copy)
        return copy

    left_hand = lhs[...].reshape(nx * nz * 16, 2 * rows)
    to_right, to_left = {"pair": right}, {"pair": left}
    core_copies, out_copies, z_copies, y_copies = [], [], [], []
    for h in range(2):
        product = dot_nn(left_hand, grad_pre[:, h * half : (h + 1) * half])
        partial[...] = product.reshape(nx, nz, 2, 8, half)
        core_out[h] = stacked(partial[:, :, 1 - core]).astype(BF16)
        core_copies.append(send(core_out.at[h], core_in.at[h], core_sem, h, to_core))
        mine[h] = stacked(partial[:, :, core])

    lo, hi = pl.ds(0, nz // 2), pl.ds(nz // 2, nz // 2)
    for h in range(2):
        core_copies[h].wait_recv()
        total = mine[h] + core_in[h].astype(F32)
        mine[h] = total
        x_out[h] = total.astype(BF16)
        out_copies.append(
            [
                send(x_out.at[h, x_far, lo], x_in.at[h, 0], x_sem, 6 * h, to_right),
                send(x_out.at[h, x_far, hi], x_in.at[h, 1], x_sem, 6 * h + 1, to_left),
                send(x_out.at[h, x_right, hi], x_in.at[h, 2], x_sem, 6 * h + 2, to_right),
                send(x_out.at[h, x_left, lo], x_in.at[h, 3], x_sem, 6 * h + 3, to_left),
            ]
        )

    for h in range(2):
        out_copies[h][0].wait_recv()
        relay_out[h, 0] = (mine[h, x_right, lo] + x_in[h, 0].astype(F32)).astype(BF16)
        copies = out_copies[h]
        copies.append(send(relay_out.at[h, 0], x_in.at[h, 4], x_sem, 6 * h + 4, to_right))
        copies[1].wait_recv()
        relay_out[h, 1] = (mine[h, x_left, hi] + x_in[h, 1].astype(F32)).astype(BF16)
        copies.append(send(relay_out.at[h, 1], x_in.at[h, 5], x_sem, 6 * h + 5, to_left))

    gf_vmem[...] = dot_nt(grad_pre[pl.ds(0, rows)], mapping[...]).astype(BF16)
    store_gf = pltpu.make_async_copy(gf_vmem, gf_hbm, local_sem.at[3])
    store_gf.start()

    for h in range(2):
        for copy in out_copies[h][2:]:
            copy.wait_recv()
        got = [x_in[h, i].astype(F32) for i in range(2, 6)]
        z_sum[h, lo] = mine[h, x_at, lo] + got[1] + got[2]
        z_sum[h, hi] = mine[h, x_at, hi] + got[0] + got[3]
        z_out[h] = z_sum[h].astype(BF16)
        z_copies.append(
            [
                send(
                    z_out.at[h, (z_at + d) % nz],
                    z_in.at[h, d - 1],
                    z_sem,
                    h * (nz - 1) + d - 1,
                    {"pair": z_mates[d - 1]},
                )
                for d in range(1, nz)
            ]
        )

    for h in range(2):
        total = z_sum[h, z_at]
        for d in range(1, nz):
            z_copies[h][d - 1].wait_recv()
            total = total + z_in[h, d - 1].astype(F32)
        y_in[h, group] = total.astype(BF16)
        y_copies.append(
            [
                send(
                    y_in.at[h, group],
                    y_in.at[h, group],
                    y_sem,
                    h * (groups - 1) + d - 1,
                    {"dp": y_groups[d - 1]},
                )
                for d in range(1, groups)
            ]
        )

    for h in range(2):
        for copy in y_copies[h]:
            copy.wait_recv()
        total = y_in[h, 0].astype(F32)
        for at in range(1, groups):
            total = total + y_in[h, at].astype(F32)
        gp_ref[:, h * half : (h + 1) * half] = jnp.concatenate([total[:8], total[8:]], axis=-1)

    store_gf.wait()
    for copy in send_feat + [send_lab, send_own] + send_theirs + sent:
        copy.wait_send()


def body(nz, nx, groups, feats, mapping, sharp, offset, segments, targets):
    rows, width = feats.shape
    half, quarter = width // 2, width // 4
    smem = pl.BlockSpec(memory_space=pltpu.SMEM)
    anywhere = pl.BlockSpec(memory_space=pl.ANY)

    def sems(n):
        return pltpu.SemaphoreType.DMA((2, n))

    return pl.pallas_call(
        functools.partial(kernel, nz, nx, groups),
        out_shape=(
            jax.ShapeDtypeStruct((rows, width), BF16),
            jax.ShapeDtypeStruct((8, width), F32),
        ),
        in_specs=[smem, smem] + [anywhere] * 4,
        out_specs=(anywhere, pl.BlockSpec(memory_space=pltpu.VMEM)),
        scratch_shapes=[
            pltpu.SMEM(segments.shape, jnp.int32),
            pltpu.VMEM((2, rows, width), BF16),
            pltpu.VMEM((2, 1, rows), jnp.int32),
            pltpu.VMEM((width, width), BF16),
            pltpu.VMEM((2, rows, width), F32),
            pltpu.VMEM((2, rows, 1), F32),
            pltpu.VMEM((4, rows, width), BF16),
            pltpu.VMEM((2, rows, width), F32),
            pltpu.VMEM((2 * rows, width), BF16),
            pltpu.VMEM((nz, nx, 2, 16, 2 * rows), BF16),
            pltpu.VMEM((nx, nz, 16, 2 * rows), BF16),
            pltpu.VMEM((nx, nz, 2, 8, half), F32),
            pltpu.VMEM((2, nx, nz, 16, quarter), F32),
            pltpu.VMEM((2, nx, nz, 16, quarter), BF16),
            pltpu.VMEM((2, nx, nz, 16, quarter), BF16),
            pltpu.VMEM((2, nx, nz, 16, quarter), BF16),
            pltpu.VMEM((2, 6, nz // 2, 16, quarter), BF16),
            pltpu.VMEM((2, 2, nz // 2, 16, quarter), BF16),
            pltpu.VMEM((2, nz, 16, quarter), F32),
            pltpu.VMEM((2, nz, 16, quarter), BF16),
            pltpu.VMEM((2, nz - 1, 16, quarter), BF16),
            pltpu.VMEM((2, groups, 16, quarter), BF16),
            pltpu.VMEM((rows, width), BF16),
            pltpu.SemaphoreType.DMA((5,)),
            sems(CHUNKS + 1),
            sems(CHUNKS + 1),
            sems(2),
            sems(12),
            sems(2 * (nz - 1)),
            sems(2 * (groups - 1)),
        ],
        compiler_params=pltpu.CompilerParams(
            collective_id=0, has_side_effects=True, vmem_limit_bytes=63 * 1024 * 1024
        ),
        cost_estimate=pl.CostEstimate(
            flops=2 * rows * width * (5 * width + 11 * rows),
            bytes_accessed=8 * rows * width,
            transcendentals=5 * rows * rows,
        ),
        name="contrastive",
    )(sharp, offset, segments, targets.reshape(1, rows), feats, mapping)


def solution(mesh, nx=NX):
    nz = mesh.shape["pair"] // (4 * nx)
    in_specs = (P(("pair", "dp"), None), P(), P(), P(), P(), P(("pair", "dp")))
    out_specs = (P(("pair", "dp"), None), P("pair", None))
    return jax.shard_map(
        functools.partial(body, nz, nx, mesh.shape["dp"]),
        mesh=mesh,
        in_specs=in_specs,
        out_specs=out_specs,
        check_vma=False,
    )
```

```python
import functools

import jax
import jax.numpy as jnp
from jax import lax
from jax.experimental import pallas as pl
from jax.experimental.pallas import tpu as pltpu
from jax.sharding import PartitionSpec as P

EPSILON = 1e-06
NX = 4
CHUNKS = 2
F32 = jnp.float32
BF16 = jnp.bfloat16


def dot_nn(a, b):
    return jnp.dot(a, b, preferred_element_type=F32)


def dot_nt(a, b):
    return lax.dot_general(a, b, (((1,), (1,)), ((), ())), preferred_element_type=F32)


def dot_tn(a, b):
    return lax.dot_general(a, b, (((0,), (0,)), ((), ())), preferred_element_type=F32)


def kernel(
    nz,
    nx,
    groups,
    sharp_ref,
    offset_ref,
    int_hbm,
    feat_hbm,
    map_hbm,
    gf_hbm,
    gp_ref,
    seg_ref,
    feats,
    labels,
    mapping,
    proj,
    inv,
    emb,
    grad_emb,
    grad_pre,
    turned,
    lhs,
    partial,
    mine,
    core_out,
    core_in,
    x_out,
    x_in,
    relay_out,
    z_sum,
    z_out,
    z_in,
    y_in,
    gf_vmem,
    local_sem,
    feat_sem,
    emb_sem,
    core_sem,
    x_sem,
    z_sem,
    y_sem,
):
    rows, width = feat_hbm.shape
    half, quarter = width // 2, width // 4
    step = rows // CHUNKS
    blocks = seg_ref.shape[1]
    pair = lax.axis_index("pair")
    group = lax.axis_index("dp")
    core = pair % 2
    y_lo = (pair // 2) % 2
    x_at = (pair // 4) % nx
    z_at = pair // (4 * nx)
    core_mate = pair + 1 - 2 * core
    y_mate = pair + 2 - 4 * y_lo
    diag_mate = y_mate + 1 - 2 * core
    x_right, x_left, x_far = (x_at + 1) % nx, (x_at + nx - 1) % nx, (x_at + 2) % nx
    right, left = pair + (x_right - x_at) * 4, pair + (x_left - x_at) * 4
    z_mates = [pair + ((z_at + d) % nz - z_at) * (4 * nx) for d in range(1, nz)]
    y_groups = [(group + d) % groups for d in range(1, groups)]
    to_core, to_y = {"pair": core_mate}, {"pair": y_mate}

    load_feat = pltpu.make_async_copy(feat_hbm, feats.at[0], local_sem.at[0])
    load_map = pltpu.make_async_copy(map_hbm, mapping, local_sem.at[1])
    load_lab = pltpu.make_async_copy(int_hbm.at[:, pl.ds(blocks, rows)], labels.at[0], local_sem.at[2])
    load_seg = pltpu.make_async_copy(int_hbm.at[:, pl.ds(0, blocks)], seg_ref, local_sem.at[4])
    loads = [load_feat, load_map, load_lab, load_seg]
    for copy in loads:
        copy.start()

    def remote(src, dst, sems, at, device):
        return pltpu.make_async_remote_copy(
            src_ref=src,
            dst_ref=dst,
            send_sem=sems.at[0, at],
            recv_sem=sems.at[1, at],
            device_id=device,
            device_id_type=pl.DeviceIdType.MESH,
        )

    barrier = pltpu.get_barrier_semaphore()
    greeted = [to_core, to_y]
    greeted += [{"pair": mate} for mate in [right, left] + z_mates]
    greeted += [{"dp": other} for other in y_groups]
    for device in greeted:
        pl.semaphore_signal(barrier, inc=1, device_id=device, device_id_type=pl.DeviceIdType.MESH)
    pl.semaphore_wait(barrier, len(greeted))

    load_feat.wait()
    load_lab.wait()
    send_lab = remote(labels.at[0], labels.at[1], feat_sem, CHUNKS, to_y)
    send_lab.start()
    send_feat = []
    for j in range(CHUNKS):
        part = pl.ds(j * step, step)
        send_feat.append(remote(feats.at[0, part], feats.at[1, part], feat_sem, j, to_y))
        send_feat[-1].start()

    mate_at, own_at, y_at, diag_at = 0, rows, 2 * rows, 3 * rows

    def embed(slot, start, size):
        part = pl.ds(start, size)
        projected = dot_nn(feats[slot, part], mapping[...])
        norm = lax.rsqrt(jnp.sum(projected * projected, axis=-1, keepdims=True) + EPSILON)
        proj[slot, part] = projected
        inv[slot, part] = norm
        emb[pl.ds((slot + 1) * rows + start, size)] = (projected * norm).astype(BF16)

    def turn(slot, start, size):
        flipped = feats[slot, pl.ds(start, size)].T.reshape(turned.shape[:4] + (size,))
        at = pl.ds(slot * rows + start, size)
        turned[:, :, :, :, at] = flipped
        for x in range(nx):
            lhs[x, :, :, at] = turned[:, x, y_lo, :, at]

    def weights(left_at, left_size, right_at, right_size, right_labels):
        left = emb[pl.ds(left_at, left_size)]
        right = emb[pl.ds(right_at, right_size)]
        logits = dot_nt(left, right) * sharp + offset
        row = lax.broadcasted_iota(jnp.int32, logits.shape, 0) + left_at
        group_row = row + firsts[left_at // rows]
        for at in range(left_at // rows + 1, (left_at + left_size - 1) // rows + 1):
            group_row = jnp.where(row < at * rows, group_row, row + firsts[at])
        hit = jnp.where(right_labels == group_row, 1.0, 0.0)
        weight = (2.0 / groups * sharp) * (jax.nn.sigmoid(logits) - hit)
        if left_at < right_at + right_size and right_at < left_at + left_size:
            column = lax.broadcasted_iota(jnp.int32, logits.shape, 1) + right_at
            weight = jnp.where(row == column, 0.0, weight)
        return weight.astype(BF16)

    def finish(slot):
        part = pl.ds(slot * rows, rows)
        grad = grad_emb[part]
        projected = proj[slot]
        norm = inv[slot]
        inner = jnp.sum(projected * grad, axis=-1, keepdims=True)
        grad_pre[part] = (norm * grad - norm**3 * inner * projected).astype(BF16)

    load_map.wait()
    embed(0, 0, rows)
    send_own = remote(emb.at[pl.ds(own_at, rows)], emb.at[pl.ds(mate_at, rows)], emb_sem, 0, to_core)
    send_own.start()
    load_seg.wait()
    sharp = sharp_ref[0]
    offset = offset_ref[0]
    held = (core_mate, pair, y_mate, diag_mate)
    firsts = [(seg_ref[0, at] - i) * rows for i, at in enumerate(held)]
    own_labels = labels[0]
    turn(0, 0, rows)
    send_own.wait_recv()
    weight = weights(mate_at, 2 * rows, own_at, rows, own_labels)
    grad_emb[pl.ds(0, rows)] = dot_tn(weight, emb[pl.ds(mate_at, 2 * rows)])

    def forward(j):
        copy = remote(
            emb.at[pl.ds(y_at + j * step, step)],
            emb.at[pl.ds(diag_at + j * step, step)],
            emb_sem,
            1 + j,
            to_core,
        )
        copy.start()
        return copy

    send_lab.wait_recv()
    their_labels = labels[1]
    send_theirs = []
    for j in range(CHUNKS):
        at = j * step
        send_feat[j].wait_recv()
        embed(1, at, step)
        send_theirs.append(forward(j))
        weight = weights(
            own_at, rows + at + step, y_at + at, step, their_labels[:, at : at + step]
        )
        earlier = pl.ds(0, rows + at)
        theirs = emb[pl.ds(y_at + at, step)]
        grad_emb[earlier] += dot_nn(weight[: rows + at], theirs)
        grad_emb[pl.ds(rows + at, step)] = dot_tn(weight, emb[pl.ds(own_at, rows + at + step)])
        turn(1, at, step)
    finish(0)
    for copy in send_theirs:
        copy.wait_recv()
    weight = weights(diag_at, rows, y_at, rows, their_labels)
    grad_emb[pl.ds(rows, rows)] += dot_tn(weight, emb[pl.ds(diag_at, rows)])
    finish(1)

    def stacked(block):
        return jnp.concatenate([block[..., :quarter], block[..., quarter:]], axis=-2)

    sent = []

    def send(src, dst, sems, at, device):
        copy = remote(src, dst, sems, at, device)
        copy.start()
        sent.append(copy)
        return copy

    def features_piece(i):
        part = pl.ds(i * quarter, quarter)
        gf_vmem[:, part] = dot_nt(grad_pre[pl.ds(0, rows)], mapping[part]).astype(BF16)

    left_hand = lhs[...].reshape(nx * nz * 16, 2 * rows)
    to_right, to_left = {"pair": right}, {"pair": left}
    core_copies, out_copies, z_copies, y_copies = [], [], [], []
    for h in range(2):
        product = dot_nn(left_hand, grad_pre[:, h * half : (h + 1) * half])
        partial[...] = product.reshape(nx, nz, 2, 8, half)
        core_out[h] = stacked(partial[:, :, 1 - core]).astype(BF16)
        core_copies.append(send(core_out.at[h], core_in.at[h], core_sem, h, to_core))
        mine[h] = stacked(partial[:, :, core])

    features_piece(0)
    lo, hi = pl.ds(0, nz // 2), pl.ds(nz // 2, nz // 2)
    for h in range(2):
        core_copies[h].wait_recv()
        total = mine[h] + core_in[h].astype(F32)
        mine[h] = total
        x_out[h] = total.astype(BF16)
        out_copies.append(
            [
                send(x_out.at[h, x_far, lo], x_in.at[h, 0], x_sem, 6 * h, to_right),
                send(x_out.at[h, x_far, hi], x_in.at[h, 1], x_sem, 6 * h + 1, to_left),
                send(x_out.at[h, x_right, hi], x_in.at[h, 2], x_sem, 6 * h + 2, to_right),
                send(x_out.at[h, x_left, lo], x_in.at[h, 3], x_sem, 6 * h + 3, to_left),
            ]
        )

    features_piece(1)
    for h in range(2):
        out_copies[h][0].wait_recv()
        relay_out[h, 0] = (mine[h, x_right, lo] + x_in[h, 0].astype(F32)).astype(BF16)
        copies = out_copies[h]
        copies.append(send(relay_out.at[h, 0], x_in.at[h, 4], x_sem, 6 * h + 4, to_right))
        copies[1].wait_recv()
        relay_out[h, 1] = (mine[h, x_left, hi] + x_in[h, 1].astype(F32)).astype(BF16)
        copies.append(send(relay_out.at[h, 1], x_in.at[h, 5], x_sem, 6 * h + 5, to_left))

    features_piece(2)
    for h in range(2):
        for copy in out_copies[h][2:]:
            copy.wait_recv()
        got = [x_in[h, i].astype(F32) for i in range(2, 6)]
        z_sum[h, lo] = mine[h, x_at, lo] + got[1] + got[2]
        z_sum[h, hi] = mine[h, x_at, hi] + got[0] + got[3]
        z_out[h] = z_sum[h].astype(BF16)
        z_copies.append(
            [
                send(
                    z_out.at[h, (z_at + d) % nz],
                    z_in.at[h, d - 1],
                    z_sem,
                    h * (nz - 1) + d - 1,
                    {"pair": z_mates[d - 1]},
                )
                for d in range(1, nz)
            ]
        )

    features_piece(3)
    store_gf = pltpu.make_async_copy(gf_vmem, gf_hbm, local_sem.at[3])
    store_gf.start()

    for h in range(2):
        total = z_sum[h, z_at]
        for d in range(1, nz):
            z_copies[h][d - 1].wait_recv()
            total = total + z_in[h, d - 1].astype(F32)
        y_in[h, group] = total.astype(BF16)
        y_copies.append(
            [
                send(
                    y_in.at[h, group],
                    y_in.at[h, group],
                    y_sem,
                    h * (groups - 1) + d - 1,
                    {"dp": y_groups[d - 1]},
                )
                for d in range(1, groups)
            ]
        )

    for h in range(2):
        for copy in y_copies[h]:
            copy.wait_recv()
        total = y_in[h, 0].astype(F32)
        for at in range(1, groups):
            total = total + y_in[h, at].astype(F32)
        gp_ref[:, h * half : (h + 1) * half] = jnp.concatenate([total[:8], total[8:]], axis=-1)

    store_gf.wait()
    for copy in send_feat + [send_lab, send_own] + send_theirs + sent:
        copy.wait_send()


def body(nz, nx, groups, feats, mapping, sharp, offset, segments, targets):
    rows, width = feats.shape
    half, quarter = width // 2, width // 4
    smem = pl.BlockSpec(memory_space=pltpu.SMEM)
    anywhere = pl.BlockSpec(memory_space=pl.ANY)

    integers = jnp.concatenate([segments.reshape(1, -1), targets.reshape(1, -1)], axis=1)

    def sems(n):
        return pltpu.SemaphoreType.DMA((2, n))

    return pl.pallas_call(
        functools.partial(kernel, nz, nx, groups),
        out_shape=(
            jax.ShapeDtypeStruct((rows, width), BF16),
            jax.ShapeDtypeStruct((8, width), F32),
        ),
        in_specs=[smem, smem] + [anywhere] * 3,
        out_specs=(anywhere, pl.BlockSpec(memory_space=pltpu.VMEM)),
        scratch_shapes=[
            pltpu.SMEM((1,) + segments.shape, jnp.int32),
            pltpu.VMEM((2, rows, width), BF16),
            pltpu.VMEM((2, 1, rows), jnp.int32),
            pltpu.VMEM((width, width), BF16),
            pltpu.VMEM((2, rows, width), F32),
            pltpu.VMEM((2, rows, 1), F32),
            pltpu.VMEM((4 * rows, width), BF16),
            pltpu.VMEM((2 * rows, width), F32),
            pltpu.VMEM((2 * rows, width), BF16),
            pltpu.VMEM((nz, nx, 2, 16, 2 * rows), BF16),
            pltpu.VMEM((nx, nz, 16, 2 * rows), BF16),
            pltpu.VMEM((nx, nz, 2, 8, half), F32),
            pltpu.VMEM((2, nx, nz, 16, quarter), F32),
            pltpu.VMEM((2, nx, nz, 16, quarter), BF16),
            pltpu.VMEM((2, nx, nz, 16, quarter), BF16),
            pltpu.VMEM((2, nx, nz, 16, quarter), BF16),
            pltpu.VMEM((2, 6, nz // 2, 16, quarter), BF16),
            pltpu.VMEM((2, 2, nz // 2, 16, quarter), BF16),
            pltpu.VMEM((2, nz, 16, quarter), F32),
            pltpu.VMEM((2, nz, 16, quarter), BF16),
            pltpu.VMEM((2, nz - 1, 16, quarter), BF16),
            pltpu.VMEM((2, groups, 16, quarter), BF16),
            pltpu.VMEM((rows, width), BF16),
            pltpu.SemaphoreType.DMA((5,)),
            sems(CHUNKS + 1),
            sems(CHUNKS + 1),
            sems(2),
            sems(12),
            sems(2 * (nz - 1)),
            sems(2 * (groups - 1)),
        ],
        compiler_params=pltpu.CompilerParams(
            collective_id=0, has_side_effects=True, vmem_limit_bytes=53 * 1024 * 1024
        ),
        cost_estimate=pl.CostEstimate(
            flops=2 * rows * width * (5 * width + 11 * rows),
            bytes_accessed=8 * rows * width,
            transcendentals=5 * rows * rows,
        ),
        name="contrastive",
    )(sharp, offset, integers, feats, mapping)


def solution(mesh, nx=NX):
    nz = mesh.shape["pair"] // (4 * nx)
    in_specs = (P(("pair", "dp"), None), P(), P(), P(), P(), P(("pair", "dp")))
    out_specs = (P(("pair", "dp"), None), P("pair", None))
    return jax.shard_map(
        functools.partial(body, nz, nx, mesh.shape["dp"]),
        mesh=mesh,
        in_specs=in_specs,
        out_specs=out_specs,
        check_vma=False,
    )
```

```python
import functools

import jax
import jax.numpy as jnp
from jax import lax
from jax.experimental import pallas as pl
from jax.experimental.pallas import tpu as pltpu
from jax.sharding import PartitionSpec as P

EPSILON = 1e-06
NX = 4
CHUNKS = 2
F32 = jnp.float32
BF16 = jnp.bfloat16


def dot_nn(a, b):
    return jnp.dot(a, b, preferred_element_type=F32)


def dot_nt(a, b):
    return lax.dot_general(a, b, (((1,), (1,)), ((), ())), preferred_element_type=F32)


def dot_tn(a, b):
    return lax.dot_general(a, b, (((0,), (0,)), ((), ())), preferred_element_type=F32)


def kernel(
    nz,
    nx,
    groups,
    sharp_ref,
    offset_ref,
    int_hbm,
    feat_hbm,
    map_hbm,
    gf_hbm,
    gp_ref,
    seg_ref,
    feats,
    labels,
    mapping,
    proj,
    inv,
    emb,
    grad_emb,
    grad_pre,
    turned,
    lhs,
    mine,
    core_out,
    core_in,
    x_out,
    x_in,
    relay_out,
    z_sum,
    z_out,
    z_in,
    y_in,
    gf_vmem,
    local_sem,
    feat_sem,
    emb_sem,
    core_sem,
    x_sem,
    z_sem,
    y_sem,
):
    rows, width = feat_hbm.shape
    half, quarter = width // 2, width // 4
    step = rows // CHUNKS
    blocks = seg_ref.shape[1]
    pair = lax.axis_index("pair")
    group = lax.axis_index("dp")
    core = pair % 2
    y_lo = (pair // 2) % 2
    x_at = (pair // 4) % nx
    z_at = pair // (4 * nx)
    core_mate = pair + 1 - 2 * core
    y_mate = pair + 2 - 4 * y_lo
    diag_mate = y_mate + 1 - 2 * core
    x_right, x_left, x_far = (x_at + 1) % nx, (x_at + nx - 1) % nx, (x_at + 2) % nx
    right, left = pair + (x_right - x_at) * 4, pair + (x_left - x_at) * 4
    z_mates = [pair + ((z_at + d) % nz - z_at) * (4 * nx) for d in range(1, nz)]
    y_groups = [(group + d) % groups for d in range(1, groups)]
    to_core, to_y = {"pair": core_mate}, {"pair": y_mate}

    load_feat = pltpu.make_async_copy(feat_hbm, feats.at[0], local_sem.at[0])
    load_map = pltpu.make_async_copy(map_hbm, mapping, local_sem.at[1])
    load_lab = pltpu.make_async_copy(int_hbm.at[:, pl.ds(blocks, rows)], labels.at[0], local_sem.at[2])
    load_seg = pltpu.make_async_copy(int_hbm.at[:, pl.ds(0, blocks)], seg_ref, local_sem.at[4])
    loads = [load_feat, load_map, load_lab, load_seg]
    for copy in loads:
        copy.start()

    def remote(src, dst, sems, at, device):
        return pltpu.make_async_remote_copy(
            src_ref=src,
            dst_ref=dst,
            send_sem=sems.at[0, at],
            recv_sem=sems.at[1, at],
            device_id=device,
            device_id_type=pl.DeviceIdType.MESH,
        )

    barrier = pltpu.get_barrier_semaphore()
    greeted = [to_core, to_y]
    greeted += [{"pair": mate} for mate in [right, left] + z_mates]
    greeted += [{"dp": other} for other in y_groups]
    for device in greeted:
        pl.semaphore_signal(barrier, inc=1, device_id=device, device_id_type=pl.DeviceIdType.MESH)
    pl.semaphore_wait(barrier, len(greeted))

    send_lab = remote(int_hbm.at[:, pl.ds(blocks, rows)], labels.at[1], feat_sem, CHUNKS, to_y)
    send_lab.start()

    send_feat = []
    for j, source in enumerate((feat_hbm, feats.at[0])):
        if j > 0:
            load_feat.wait()
        part = pl.ds(j * step, step)
        send_feat.append(remote(source.at[part], feats.at[1, part], feat_sem, j, to_y))
        send_feat[-1].start()

    mate_at, own_at, y_at, diag_at = 0, rows, 2 * rows, 3 * rows

    def embed(slot, start, size):
        part = pl.ds(start, size)
        projected = dot_nn(feats[slot, part], mapping[...])
        norm = lax.rsqrt(jnp.sum(projected * projected, axis=-1, keepdims=True) + EPSILON)
        proj[slot, part] = projected
        inv[slot, part] = norm
        emb[pl.ds((slot + 1) * rows + start, size)] = (projected * norm).astype(BF16)

    def turn(slot, start, size):
        flipped = feats[slot, pl.ds(start, size)].astype(F32).T
        at = pl.ds(slot * rows + start, size)
        turned[:, :, :, :, :, at] = flipped.reshape(turned.shape[:5] + (size,))
        for i, owner in enumerate((1 - core, core)):
            for x in range(nx):
                block = turned[:, x, y_lo, owner, :, at].reshape(nz * 8, size)
                lhs[i, pl.ds(x * nz * 8, nz * 8), at] = block.astype(BF16)

    def weights(left_at, left_size, right_at, right_size, right_labels):
        left = emb[pl.ds(left_at, left_size)]
        right = emb[pl.ds(right_at, right_size)]
        logits = dot_nt(left, right) * sharp + offset
        row = lax.broadcasted_iota(jnp.int32, logits.shape, 0) + left_at
        group_row = row + firsts[left_at // rows]
        for at in range(left_at // rows + 1, (left_at + left_size - 1) // rows + 1):
            group_row = jnp.where(row < at * rows, group_row, row + firsts[at])
        hit = jnp.where(right_labels == group_row, 1.0, 0.0)
        weight = (2.0 / groups * sharp) * (jax.nn.sigmoid(logits) - hit)
        if left_at < right_at + right_size and right_at < left_at + left_size:
            column = lax.broadcasted_iota(jnp.int32, logits.shape, 1) + right_at
            weight = jnp.where(row == column, 0.0, weight)
        return weight.astype(BF16)

    def finish(slot):
        part = pl.ds(slot * rows, rows)
        grad = grad_emb[part]
        projected = proj[slot]
        norm = inv[slot]
        inner = jnp.sum(projected * grad, axis=-1, keepdims=True)
        grad_pre[part] = (norm * grad - norm**3 * inner * projected).astype(BF16)

    load_map.wait()
    embed(0, 0, rows)
    send_own = remote(emb.at[pl.ds(own_at, rows)], emb.at[pl.ds(mate_at, rows)], emb_sem, 0, to_core)
    send_own.start()
    load_seg.wait()
    load_lab.wait()
    sharp = sharp_ref[0]
    offset = offset_ref[0]
    held = (core_mate, pair, y_mate, diag_mate)
    firsts = [(seg_ref[0, at] - i) * rows for i, at in enumerate(held)]
    own_labels = labels[0]
    turn(0, 0, rows)
    send_own.wait_recv()
    weight = weights(mate_at, 2 * rows, own_at, rows, own_labels)
    grad_emb[pl.ds(0, rows)] = dot_tn(weight, emb[pl.ds(mate_at, 2 * rows)])

    def forward(j):
        copy = remote(
            emb.at[pl.ds(y_at + j * step, step)],
            emb.at[pl.ds(diag_at + j * step, step)],
            emb_sem,
            1 + j,
            to_core,
        )
        copy.start()
        return copy

    send_lab.wait_recv()
    their_labels = labels[1]
    send_theirs = []
    for j in range(CHUNKS):
        at = j * step
        send_feat[j].wait_recv()
        embed(1, at, step)
        send_theirs.append(forward(j))
        weight = weights(
            own_at, rows + at + step, y_at + at, step, their_labels[:, at : at + step]
        )
        earlier = pl.ds(0, rows + at)
        theirs = emb[pl.ds(y_at + at, step)]
        grad_emb[earlier] += dot_nn(weight[: rows + at], theirs)
        grad_emb[pl.ds(rows + at, step)] = dot_tn(weight, emb[pl.ds(own_at, rows + at + step)])
        turn(1, at, step)
    finish(0)
    for copy in send_theirs:
        copy.wait_recv()
    weight = weights(diag_at, rows, y_at, rows, their_labels)
    grad_emb[pl.ds(rows, rows)] += dot_tn(weight, emb[pl.ds(diag_at, rows)])
    finish(1)

    def product(i, h):
        block = dot_nn(lhs[i], grad_pre[:, h * half : (h + 1) * half])
        block = block.reshape(nx, nz, 8, half)
        return jnp.concatenate([block[..., :quarter], block[..., quarter:]], axis=-2)

    sent = []

    def send(src, dst, sems, at, device):
        copy = remote(src, dst, sems, at, device)
        copy.start()
        sent.append(copy)
        return copy

    def features_piece(i):
        part = pl.ds(i * quarter, quarter)
        gf_vmem[:, part] = dot_nt(grad_pre[pl.ds(0, rows)], mapping[part]).astype(BF16)

    to_right, to_left = {"pair": right}, {"pair": left}
    core_copies, out_copies, z_copies, y_copies = [], [], [], []
    for h in range(2):
        core_out[h] = product(0, h).astype(BF16)
        core_copies.append(send(core_out.at[h], core_in.at[h], core_sem, h, to_core))
    for h in range(2):
        mine[h] = product(1, h)

    lo, hi = pl.ds(0, nz // 2), pl.ds(nz // 2, nz // 2)

    def send_x(h, i, src):
        return send(src, x_in.at[h, i], x_sem, 6 * h + i, to_left if i % 2 else to_right)

    def send_far(h):
        core_copies[h].wait_recv()
        total = mine[h] + core_in[h].astype(F32)
        mine[h] = total
        x_out[h] = total.astype(BF16)
        out_copies.append([send_x(h, 0, x_out.at[h, x_far, lo]), send_x(h, 1, x_out.at[h, x_far, hi])])

    def send_direct(h):
        out_copies[h].append(send_x(h, 2, x_out.at[h, x_right, hi]))
        out_copies[h].append(send_x(h, 3, x_out.at[h, x_left, lo]))

    def relay(h):
        for i, (x, part) in enumerate(((x_right, lo), (x_left, hi))):
            out_copies[h][i].wait_recv()
            relay_out[h, i] = (mine[h, x, part] + x_in[h, i].astype(F32)).astype(BF16)
            out_copies[h].append(send_x(h, 4 + i, relay_out.at[h, i]))

    features_piece(0)
    send_far(0)
    send_far(1)
    send_direct(0)
    features_piece(1)
    relay(0)
    send_direct(1)
    relay(1)
    features_piece(2)
    for h in range(2):
        for copy in out_copies[h][2:]:
            copy.wait_recv()
        got = [x_in[h, i].astype(F32) for i in range(2, 6)]
        z_sum[h, lo] = mine[h, x_at, lo] + got[1] + got[2]
        z_sum[h, hi] = mine[h, x_at, hi] + got[0] + got[3]
        z_out[h] = z_sum[h].astype(BF16)
        z_copies.append(
            [
                send(
                    z_out.at[h, (z_at + d) % nz],
                    z_in.at[h, d - 1],
                    z_sem,
                    h * (nz - 1) + d - 1,
                    {"pair": z_mates[d - 1]},
                )
                for d in range(1, nz)
            ]
        )

    features_piece(3)
    store_gf = pltpu.make_async_copy(gf_vmem, gf_hbm, local_sem.at[3])
    store_gf.start()

    for h in range(2):
        total = z_sum[h, z_at]
        for d in range(1, nz):
            z_copies[h][d - 1].wait_recv()
            total = total + z_in[h, d - 1].astype(F32)
        y_in[h, group] = total.astype(BF16)
        y_copies.append(
            [
                send(
                    y_in.at[h, group],
                    y_in.at[h, group],
                    y_sem,
                    h * (groups - 1) + d - 1,
                    {"dp": y_groups[d - 1]},
                )
                for d in range(1, groups)
            ]
        )

    for h in range(2):
        for copy in y_copies[h]:
            copy.wait_recv()
        total = y_in[h, 0].astype(F32)
        for at in range(1, groups):
            total = total + y_in[h, at].astype(F32)
        gp_ref[:, h * half : (h + 1) * half] = jnp.concatenate([total[:8], total[8:]], axis=-1)

    store_gf.wait()
    for copy in send_feat + [send_lab, send_own] + send_theirs + sent:
        copy.wait_send()


def body(nz, nx, groups, feats, mapping, sharp, offset, segments, targets):
    rows, width = feats.shape
    half, quarter = width // 2, width // 4
    smem = pl.BlockSpec(memory_space=pltpu.SMEM)
    anywhere = pl.BlockSpec(memory_space=pl.ANY)

    integers = jnp.concatenate([segments.reshape(1, -1), targets.reshape(1, -1)], axis=1)

    def sems(n):
        return pltpu.SemaphoreType.DMA((2, n))

    return pl.pallas_call(
        functools.partial(kernel, nz, nx, groups),
        out_shape=(
            jax.ShapeDtypeStruct((rows, width), BF16),
            jax.ShapeDtypeStruct((8, width), F32),
        ),
        in_specs=[smem, smem] + [anywhere] * 3,
        out_specs=(anywhere, pl.BlockSpec(memory_space=pltpu.VMEM)),
        scratch_shapes=[
            pltpu.SMEM((1,) + segments.shape, jnp.int32),
            pltpu.VMEM((2, rows, width), BF16),
            pltpu.VMEM((2, 1, rows), jnp.int32),
            pltpu.VMEM((width, width), BF16),
            pltpu.VMEM((2, rows, width), F32),
            pltpu.VMEM((2, rows, 1), F32),
            pltpu.VMEM((4 * rows, width), BF16),
            pltpu.VMEM((2 * rows, width), F32),
            pltpu.VMEM((2 * rows, width), BF16),
            pltpu.VMEM((nz, nx, 2, 2, 8, 2 * rows), F32),
            pltpu.VMEM((2, nx * nz * 8, 2 * rows), BF16),
            pltpu.VMEM((2, nx, nz, 16, quarter), F32),
            pltpu.VMEM((2, nx, nz, 16, quarter), BF16),
            pltpu.VMEM((2, nx, nz, 16, quarter), BF16),
            pltpu.VMEM((2, nx, nz, 16, quarter), BF16),
            pltpu.VMEM((2, 6, nz // 2, 16, quarter), BF16),
            pltpu.VMEM((2, 2, nz // 2, 16, quarter), BF16),
            pltpu.VMEM((2, nz, 16, quarter), F32),
            pltpu.VMEM((2, nz, 16, quarter), BF16),
            pltpu.VMEM((2, nz - 1, 16, quarter), BF16),
            pltpu.VMEM((2, groups, 16, quarter), BF16),
            pltpu.VMEM((rows, width), BF16),
            pltpu.SemaphoreType.DMA((5,)),
            sems(CHUNKS + 1),
            sems(CHUNKS + 1),
            sems(2),
            sems(12),
            sems(2 * (nz - 1)),
            sems(2 * (groups - 1)),
        ],
        compiler_params=pltpu.CompilerParams(
            collective_id=0, has_side_effects=True, vmem_limit_bytes=53 * 1024 * 1024
        ),
        cost_estimate=pl.CostEstimate(
            flops=2 * rows * width * (5 * width + 11 * rows),
            bytes_accessed=8 * rows * width,
            transcendentals=5 * rows * rows,
        ),
        name="contrastive",
    )(sharp, offset, integers, feats, mapping)


def solution(mesh, nx=NX):
    nz = mesh.shape["pair"] // (4 * nx)
    in_specs = (P(("pair", "dp"), None), P(), P(), P(), P(), P(("pair", "dp")))
    out_specs = (P(("pair", "dp"), None), P("pair", None))
    return jax.shard_map(
        functools.partial(body, nz, nx, mesh.shape["dp"]),
        mesh=mesh,
        in_specs=in_specs,
        out_specs=out_specs,
        check_vma=False,
    )
```

```python
import functools

import jax
import jax.numpy as jnp
from jax import lax
from jax.experimental import pallas as pl
from jax.experimental.pallas import tpu as pltpu
from jax.sharding import PartitionSpec as P

EPSILON = 1e-06
NX = 4
CHUNKS = 2
F32 = jnp.float32
BF16 = jnp.bfloat16


def dot_nn(a, b):
    return jnp.dot(a, b, preferred_element_type=F32)


def dot_nt(a, b):
    return lax.dot_general(a, b, (((1,), (1,)), ((), ())), preferred_element_type=F32)


def dot_tn(a, b):
    return lax.dot_general(a, b, (((0,), (0,)), ((), ())), preferred_element_type=F32)


def kernel(
    nz,
    nx,
    groups,
    sharp_ref,
    offset_ref,
    int_hbm,
    feat_hbm,
    map_hbm,
    gf_hbm,
    gp_ref,
    seg_ref,
    feats,
    labels,
    mapping,
    flipped_map,
    proj,
    inv,
    emb,
    grad_emb,
    grad_pre,
    turned,
    lhs,
    mine,
    core_out,
    core_in,
    x_out,
    x_in,
    relay_out,
    z_sum,
    z_out,
    z_in,
    y_in,
    gf_vmem,
    local_sem,
    feat_sem,
    emb_sem,
    core_sem,
    x_sem,
    z_sem,
    y_sem,
):
    rows, width = feat_hbm.shape
    half, quarter = width // 2, width // 4
    step = rows // CHUNKS
    blocks = seg_ref.shape[1]
    pair = lax.axis_index("pair")
    group = lax.axis_index("dp")
    core = pair % 2
    y_lo = (pair // 2) % 2
    x_at = (pair // 4) % nx
    z_at = pair // (4 * nx)
    core_mate = pair + 1 - 2 * core
    y_mate = pair + 2 - 4 * y_lo
    diag_mate = y_mate + 1 - 2 * core
    x_right, x_left, x_far = (x_at + 1) % nx, (x_at + nx - 1) % nx, (x_at + 2) % nx
    right, left = pair + (x_right - x_at) * 4, pair + (x_left - x_at) * 4
    z_mates = [pair + ((z_at + d) % nz - z_at) * (4 * nx) for d in range(1, nz)]
    y_groups = [(group + d) % groups for d in range(1, groups)]
    to_core, to_y = {"pair": core_mate}, {"pair": y_mate}

    load_feat = pltpu.make_async_copy(feat_hbm, feats.at[0], local_sem.at[0])
    load_map = pltpu.make_async_copy(map_hbm, mapping, local_sem.at[1])
    load_lab = pltpu.make_async_copy(int_hbm.at[:, pl.ds(blocks, rows)], labels.at[0], local_sem.at[2])
    load_seg = pltpu.make_async_copy(int_hbm.at[:, pl.ds(0, blocks)], seg_ref, local_sem.at[4])
    loads = [load_feat, load_map, load_lab, load_seg]
    for copy in loads:
        copy.start()

    def remote(src, dst, sems, at, device):
        return pltpu.make_async_remote_copy(
            src_ref=src,
            dst_ref=dst,
            send_sem=sems.at[0, at],
            recv_sem=sems.at[1, at],
            device_id=device,
            device_id_type=pl.DeviceIdType.MESH,
        )

    barrier = pltpu.get_barrier_semaphore()
    greeted = [to_core, to_y]
    greeted += [{"pair": mate} for mate in [right, left] + z_mates]
    greeted += [{"dp": other} for other in y_groups]
    for device in greeted:
        pl.semaphore_signal(barrier, inc=1, device_id=device, device_id_type=pl.DeviceIdType.MESH)
    pl.semaphore_wait(barrier, len(greeted))

    send_lab = remote(int_hbm.at[:, pl.ds(blocks, rows)], labels.at[1], feat_sem, CHUNKS, to_y)
    send_lab.start()

    send_feat = []
    for j, source in enumerate((feat_hbm, feats.at[0])):
        if j > 0:
            load_feat.wait()
        part = pl.ds(j * step, step)
        send_feat.append(remote(source.at[part], feats.at[1, part], feat_sem, j, to_y))
        send_feat[-1].start()

    mate_at, own_at, y_at, diag_at = 0, rows, 2 * rows, 3 * rows

    def embed(slot, start, size):
        part = pl.ds(start, size)
        projected = dot_nn(feats[slot, part], mapping[...])
        norm = lax.rsqrt(jnp.sum(projected * projected, axis=-1, keepdims=True) + EPSILON)
        proj[slot, part] = projected
        inv[slot, part] = norm
        emb[pl.ds((slot + 1) * rows + start, size)] = (projected * norm).astype(BF16)

    def turn(slot, start, size):
        flipped = feats[slot, pl.ds(start, size)].astype(F32).T
        at = pl.ds(slot * rows + start, size)
        turned[:, :, :, :, :, at] = flipped.reshape(turned.shape[:5] + (size,))
        for i, owner in enumerate((1 - core, core)):
            for x in range(nx):
                block = turned[:, x, y_lo, owner, :, at].reshape(nz * 8, size)
                lhs[i, pl.ds(x * nz * 8, nz * 8), at] = block.astype(BF16)

    def weights(left_at, left_size, right_at, right_size, right_labels):
        left = emb[pl.ds(left_at, left_size)]
        right = emb[pl.ds(right_at, right_size)]
        logits = dot_nt(left, right) * sharp + offset
        row = lax.broadcasted_iota(jnp.int32, logits.shape, 0) + left_at
        group_row = row + firsts[left_at // rows]
        for at in range(left_at // rows + 1, (left_at + left_size - 1) // rows + 1):
            group_row = jnp.where(row < at * rows, group_row, row + firsts[at])
        hit = jnp.where(right_labels == group_row, 1.0, 0.0)
        weight = (2.0 / groups * sharp) * (jax.nn.sigmoid(logits) - hit)
        if left_at < right_at + right_size and right_at < left_at + left_size:
            column = lax.broadcasted_iota(jnp.int32, logits.shape, 1) + right_at
            weight = jnp.where(row == column, 0.0, weight)
        return weight.astype(BF16)

    def finish(slot):
        part = pl.ds(slot * rows, rows)
        grad = grad_emb[part]
        projected = proj[slot]
        norm = inv[slot]
        inner = jnp.sum(projected * grad, axis=-1, keepdims=True)
        grad_pre[part] = (norm * grad - norm**3 * inner * projected).astype(BF16)

    load_map.wait()
    embed(0, 0, rows)
    send_own = remote(emb.at[pl.ds(own_at, rows)], emb.at[pl.ds(mate_at, rows)], emb_sem, 0, to_core)
    send_own.start()
    load_seg.wait()
    load_lab.wait()
    sharp = sharp_ref[0]
    offset = offset_ref[0]
    held = (core_mate, pair, y_mate, diag_mate)
    firsts = [(seg_ref[0, at] - i) * rows for i, at in enumerate(held)]
    own_labels = labels[0]
    turn(0, 0, rows)
    send_own.wait_recv()
    weight = weights(mate_at, 2 * rows, own_at, rows, own_labels)
    grad_emb[pl.ds(0, rows)] = dot_tn(weight, emb[pl.ds(mate_at, 2 * rows)])

    def forward(j):
        copy = remote(
            emb.at[pl.ds(y_at + j * step, step)],
            emb.at[pl.ds(diag_at + j * step, step)],
            emb_sem,
            1 + j,
            to_core,
        )
        copy.start()
        return copy

    send_lab.wait_recv()
    their_labels = labels[1]
    send_theirs = []
    for j in range(CHUNKS):
        at = j * step
        send_feat[j].wait_recv()
        embed(1, at, step)
        send_theirs.append(forward(j))
        weight = weights(
            own_at, rows + at + step, y_at + at, step, their_labels[:, at : at + step]
        )
        earlier = pl.ds(0, rows + at)
        theirs = emb[pl.ds(y_at + at, step)]
        grad_emb[earlier] += dot_nn(weight[: rows + at], theirs)
        grad_emb[pl.ds(rows + at, step)] = dot_tn(weight, emb[pl.ds(own_at, rows + at + step)])
        turn(1, at, step)
        if j == 0:
            for k in range(4):
                part = pl.ds(k * quarter, quarter)
                flipped_map[:, part] = mapping[part].T
    finish(0)
    for copy in send_theirs:
        copy.wait_recv()
    weight = weights(diag_at, rows, y_at, rows, their_labels)
    grad_emb[pl.ds(rows, rows)] += dot_tn(weight, emb[pl.ds(diag_at, rows)])
    finish(1)

    def product(i, h):
        block = dot_nn(lhs[i], grad_pre[:, h * half : (h + 1) * half])
        block = block.reshape(nx, nz, 8, half)
        return jnp.concatenate([block[..., :quarter], block[..., quarter:]], axis=-2)

    sent = []

    def send(src, dst, sems, at, device):
        copy = remote(src, dst, sems, at, device)
        copy.start()
        sent.append(copy)
        return copy

    to_right, to_left = {"pair": right}, {"pair": left}
    core_copies, out_copies, z_copies, y_copies = [], [], [], []
    for h in range(2):
        core_out[h] = product(0, h).astype(BF16)
        core_copies.append(send(core_out.at[h], core_in.at[h], core_sem, h, to_core))
    for h in range(2):
        mine[h] = product(1, h)

    lo, hi = pl.ds(0, nz // 2), pl.ds(nz // 2, nz // 2)

    def send_x(h, i, src):
        return send(src, x_in.at[h, i], x_sem, 6 * h + i, to_left if i % 2 else to_right)

    def send_far(h):
        core_copies[h].wait_recv()
        total = mine[h] + core_in[h].astype(F32)
        mine[h] = total
        x_out[h] = total.astype(BF16)
        out_copies.append([send_x(h, 0, x_out.at[h, x_far, lo]), send_x(h, 1, x_out.at[h, x_far, hi])])

    def send_direct(h):
        out_copies[h].append(send_x(h, 2, x_out.at[h, x_right, hi]))
        out_copies[h].append(send_x(h, 3, x_out.at[h, x_left, lo]))

    def relay(h):
        for i, (x, part) in enumerate(((x_right, lo), (x_left, hi))):
            out_copies[h][i].wait_recv()
            relay_out[h, i] = (mine[h, x, part] + x_in[h, i].astype(F32)).astype(BF16)
            out_copies[h].append(send_x(h, 4 + i, relay_out.at[h, i]))

    send_far(0)
    send_far(1)
    send_direct(0)
    relay(0)
    send_direct(1)
    relay(1)
    for h in range(2):
        for copy in out_copies[h][2:]:
            copy.wait_recv()
        got = [x_in[h, i].astype(F32) for i in range(2, 6)]
        z_sum[h, lo] = mine[h, x_at, lo] + got[1] + got[2]
        z_sum[h, hi] = mine[h, x_at, hi] + got[0] + got[3]
        z_out[h] = z_sum[h].astype(BF16)
        z_copies.append(
            [
                send(
                    z_out.at[h, (z_at + d) % nz],
                    z_in.at[h, d - 1],
                    z_sem,
                    h * (nz - 1) + d - 1,
                    {"pair": z_mates[d - 1]},
                )
                for d in range(1, nz)
            ]
        )

    for h in range(2):
        total = z_sum[h, z_at]
        for d in range(1, nz):
            z_copies[h][d - 1].wait_recv()
            total = total + z_in[h, d - 1].astype(F32)
        y_in[h, group] = total.astype(BF16)
        y_copies.append(
            [
                send(
                    y_in.at[h, group],
                    y_in.at[h, group],
                    y_sem,
                    h * (groups - 1) + d - 1,
                    {"dp": y_groups[d - 1]},
                )
                for d in range(1, groups)
            ]
        )

    gf_vmem[...] = dot_nn(grad_pre[pl.ds(0, rows)], flipped_map[...]).astype(BF16)
    store_gf = pltpu.make_async_copy(gf_vmem, gf_hbm, local_sem.at[3])
    store_gf.start()

    for h in range(2):
        for copy in y_copies[h]:
            copy.wait_recv()
        total = y_in[h, 0].astype(F32)
        for at in range(1, groups):
            total = total + y_in[h, at].astype(F32)
        gp_ref[:, h * half : (h + 1) * half] = jnp.concatenate([total[:8], total[8:]], axis=-1)

    store_gf.wait()
    for copy in send_feat + [send_lab, send_own] + send_theirs + sent:
        copy.wait_send()


def body(nz, nx, groups, feats, mapping, sharp, offset, segments, targets):
    rows, width = feats.shape
    half, quarter = width // 2, width // 4
    smem = pl.BlockSpec(memory_space=pltpu.SMEM)
    anywhere = pl.BlockSpec(memory_space=pl.ANY)

    integers = jnp.concatenate([segments.reshape(1, -1), targets.reshape(1, -1)], axis=1)

    def sems(n):
        return pltpu.SemaphoreType.DMA((2, n))

    return pl.pallas_call(
        functools.partial(kernel, nz, nx, groups),
        out_shape=(
            jax.ShapeDtypeStruct((rows, width), BF16),
            jax.ShapeDtypeStruct((8, width), F32),
        ),
        in_specs=[smem, smem] + [anywhere] * 3,
        out_specs=(anywhere, pl.BlockSpec(memory_space=pltpu.VMEM)),
        scratch_shapes=[
            pltpu.SMEM((1,) + segments.shape, jnp.int32),
            pltpu.VMEM((2, rows, width), BF16),
            pltpu.VMEM((2, 1, rows), jnp.int32),
            pltpu.VMEM((width, width), BF16),
            pltpu.VMEM((width, width), BF16),
            pltpu.VMEM((2, rows, width), F32),
            pltpu.VMEM((2, rows, 1), F32),
            pltpu.VMEM((4 * rows, width), BF16),
            pltpu.VMEM((2 * rows, width), F32),
            pltpu.VMEM((2 * rows, width), BF16),
            pltpu.VMEM((nz, nx, 2, 2, 8, 2 * rows), F32),
            pltpu.VMEM((2, nx * nz * 8, 2 * rows), BF16),
            pltpu.VMEM((2, nx, nz, 16, quarter), F32),
            pltpu.VMEM((2, nx, nz, 16, quarter), BF16),
            pltpu.VMEM((2, nx, nz, 16, quarter), BF16),
            pltpu.VMEM((2, nx, nz, 16, quarter), BF16),
            pltpu.VMEM((2, 6, nz // 2, 16, quarter), BF16),
            pltpu.VMEM((2, 2, nz // 2, 16, quarter), BF16),
            pltpu.VMEM((2, nz, 16, quarter), F32),
            pltpu.VMEM((2, nz, 16, quarter), BF16),
            pltpu.VMEM((2, nz - 1, 16, quarter), BF16),
            pltpu.VMEM((2, groups, 16, quarter), BF16),
            pltpu.VMEM((rows, width), BF16),
            pltpu.SemaphoreType.DMA((5,)),
            sems(CHUNKS + 1),
            sems(CHUNKS + 1),
            sems(2),
            sems(12),
            sems(2 * (nz - 1)),
            sems(2 * (groups - 1)),
        ],
        compiler_params=pltpu.CompilerParams(
            collective_id=0, has_side_effects=True, vmem_limit_bytes=53 * 1024 * 1024
        ),
        cost_estimate=pl.CostEstimate(
            flops=2 * rows * width * (5 * width + 11 * rows),
            bytes_accessed=8 * rows * width,
            transcendentals=5 * rows * rows,
        ),
        name="contrastive",
    )(sharp, offset, integers, feats, mapping)


def solution(mesh, nx=NX):
    nz = mesh.shape["pair"] // (4 * nx)
    in_specs = (P(("pair", "dp"), None), P(), P(), P(), P(), P(("pair", "dp")))
    out_specs = (P(("pair", "dp"), None), P("pair", None))
    return jax.shard_map(
        functools.partial(body, nz, nx, mesh.shape["dp"]),
        mesh=mesh,
        in_specs=in_specs,
        out_specs=out_specs,
        check_vma=False,
    )
```

```python
import functools

import jax
import jax.numpy as jnp
from jax import lax
from jax.experimental import pallas as pl
from jax.experimental.pallas import tpu as pltpu
from jax.sharding import PartitionSpec as P

EPSILON = 1e-06
NX = 4
CHUNKS = 2
F32 = jnp.float32
BF16 = jnp.bfloat16


def dot_nn(a, b):
    return jnp.dot(a, b, preferred_element_type=F32)


def dot_nt(a, b):
    return lax.dot_general(a, b, (((1,), (1,)), ((), ())), preferred_element_type=F32)


def dot_tn(a, b):
    return lax.dot_general(a, b, (((0,), (0,)), ((), ())), preferred_element_type=F32)


def kernel(
    nz,
    nx,
    groups,
    sharp_ref,
    offset_ref,
    int_hbm,
    feat_hbm,
    map_hbm,
    gf_hbm,
    gp_ref,
    seg_ref,
    feats,
    labels,
    mapping,
    flipped_map,
    proj,
    inv,
    emb,
    grad_emb,
    grad_pre,
    turned,
    lhs,
    mine,
    core_out,
    core_in,
    x_out,
    x_in,
    relay_out,
    z_sum,
    z_out,
    z_in,
    y_in,
    gf_vmem,
    local_sem,
    feat_sem,
    emb_sem,
    core_sem,
    x_sem,
    z_sem,
    y_sem,
    z_token,
    y_token,
):
    rows, width = feat_hbm.shape
    half, quarter = width // 2, width // 4
    step = rows // CHUNKS
    blocks = seg_ref.shape[1]
    pair = lax.axis_index("pair")
    group = lax.axis_index("dp")
    core = pair % 2
    y_lo = (pair // 2) % 2
    x_at = (pair // 4) % nx
    z_at = pair // (4 * nx)
    core_mate = pair + 1 - 2 * core
    y_mate = pair + 2 - 4 * y_lo
    diag_mate = y_mate + 1 - 2 * core
    x_right, x_left, x_far = (x_at + 1) % nx, (x_at + nx - 1) % nx, (x_at + 2) % nx
    right, left = pair + (x_right - x_at) * 4, pair + (x_left - x_at) * 4
    z_mates = [pair + ((z_at + d) % nz - z_at) * (4 * nx) for d in range(1, nz)]
    y_groups = [(group + d) % groups for d in range(1, groups)]
    to_core, to_y = {"pair": core_mate}, {"pair": y_mate}

    load_feat = pltpu.make_async_copy(feat_hbm, feats.at[0], local_sem.at[0])
    load_map = pltpu.make_async_copy(map_hbm, mapping, local_sem.at[1])
    load_lab = pltpu.make_async_copy(int_hbm.at[:, pl.ds(blocks, rows)], labels.at[0], local_sem.at[2])
    load_seg = pltpu.make_async_copy(int_hbm.at[:, pl.ds(0, blocks)], seg_ref, local_sem.at[4])
    loads = [load_feat, load_map, load_lab, load_seg]
    for copy in loads:
        copy.start()

    def remote(src, dst, sems, at, device):
        return pltpu.make_async_remote_copy(
            src_ref=src,
            dst_ref=dst,
            send_sem=sems.at[0, at],
            recv_sem=sems.at[1, at],
            device_id=device,
            device_id_type=pl.DeviceIdType.MESH,
        )

    barrier = pltpu.get_barrier_semaphore()
    z_near = [{"pair": z_mates[0]}, {"pair": z_mates[-1]}]
    greeted = [to_core, to_y, {"pair": right}, {"pair": left}] + z_near
    greeted += [{"dp": y_groups[0]}, {"dp": y_groups[-1]}]
    for device in greeted:
        pl.semaphore_signal(barrier, inc=1, device_id=device, device_id_type=pl.DeviceIdType.MESH)
    pl.semaphore_wait(barrier, len(greeted))

    def pass_on(i):
        for side in range(2):
            pl.semaphore_signal(
                z_token.at[i, side],
                inc=1,
                device_id=z_near[side],
                device_id_type=pl.DeviceIdType.MESH,
            )

    def heard(i):
        for side in range(2):
            pl.semaphore_wait(z_token.at[i, side], 1)

    tokens = nz // 2 - 1
    if tokens > 0:
        pass_on(0)
    pl.semaphore_signal(
        y_token, inc=1, device_id={"dp": y_groups[0]}, device_id_type=pl.DeviceIdType.MESH
    )

    send_lab = remote(int_hbm.at[:, pl.ds(blocks, rows)], labels.at[1], feat_sem, CHUNKS, to_y)
    send_lab.start()

    send_feat = []
    for j, source in enumerate((feat_hbm, feats.at[0])):
        if j > 0:
            load_feat.wait()
        part = pl.ds(j * step, step)
        send_feat.append(remote(source.at[part], feats.at[1, part], feat_sem, j, to_y))
        send_feat[-1].start()

    mate_at, own_at, y_at, diag_at = 0, rows, 2 * rows, 3 * rows

    def embed(slot, start, size):
        part = pl.ds(start, size)
        projected = dot_nn(feats[slot, part], mapping[...])
        norm = lax.rsqrt(jnp.sum(projected * projected, axis=-1, keepdims=True) + EPSILON)
        proj[slot, part] = projected
        inv[slot, part] = norm
        emb[pl.ds((slot + 1) * rows + start, size)] = (projected * norm).astype(BF16)

    def turn(slot, start, size):
        flipped = feats[slot, pl.ds(start, size)].astype(F32).T
        at = pl.ds(slot * rows + start, size)
        turned[:, :, :, :, :, at] = flipped.reshape(turned.shape[:5] + (size,))
        for i, owner in enumerate((1 - core, core)):
            for x in range(nx):
                block = turned[:, x, y_lo, owner, :, at].reshape(nz * 8, size)
                lhs[i, pl.ds(x * nz * 8, nz * 8), at] = block.astype(BF16)

    def weights(left_at, left_size, right_at, right_size, right_labels):
        left = emb[pl.ds(left_at, left_size)]
        right = emb[pl.ds(right_at, right_size)]
        logits = dot_nt(left, right) * sharp + offset
        row = lax.broadcasted_iota(jnp.int32, logits.shape, 0) + left_at
        group_row = row + firsts[left_at // rows]
        for at in range(left_at // rows + 1, (left_at + left_size - 1) // rows + 1):
            group_row = jnp.where(row < at * rows, group_row, row + firsts[at])
        hit = jnp.where(right_labels == group_row, 1.0, 0.0)
        weight = (2.0 / groups * sharp) * (jax.nn.sigmoid(logits) - hit)
        if left_at < right_at + right_size and right_at < left_at + left_size:
            column = lax.broadcasted_iota(jnp.int32, logits.shape, 1) + right_at
            weight = jnp.where(row == column, 0.0, weight)
        return weight.astype(BF16)

    def finish(slot):
        part = pl.ds(slot * rows, rows)
        grad = grad_emb[part]
        projected = proj[slot]
        norm = inv[slot]
        inner = jnp.sum(projected * grad, axis=-1, keepdims=True)
        grad_pre[part] = (norm * grad - norm**3 * inner * projected).astype(BF16)

    load_map.wait()
    embed(0, 0, rows)
    send_own = remote(emb.at[pl.ds(own_at, rows)], emb.at[pl.ds(mate_at, rows)], emb_sem, 0, to_core)
    send_own.start()
    load_seg.wait()
    load_lab.wait()
    sharp = sharp_ref[0]
    offset = offset_ref[0]
    held = (core_mate, pair, y_mate, diag_mate)
    firsts = [(seg_ref[0, at] - i) * rows for i, at in enumerate(held)]
    own_labels = labels[0]
    turn(0, 0, rows)
    if tokens > 1:
        heard(0)
        pass_on(1)
    send_own.wait_recv()
    weight = weights(mate_at, 2 * rows, own_at, rows, own_labels)
    grad_emb[pl.ds(0, rows)] = dot_tn(weight, emb[pl.ds(mate_at, 2 * rows)])

    def forward(j):
        copy = remote(
            emb.at[pl.ds(y_at + j * step, step)],
            emb.at[pl.ds(diag_at + j * step, step)],
            emb_sem,
            1 + j,
            to_core,
        )
        copy.start()
        return copy

    send_lab.wait_recv()
    their_labels = labels[1]
    send_theirs = []
    for j in range(CHUNKS):
        at = j * step
        send_feat[j].wait_recv()
        embed(1, at, step)
        send_theirs.append(forward(j))
        weight = weights(
            own_at, rows + at + step, y_at + at, step, their_labels[:, at : at + step]
        )
        earlier = pl.ds(0, rows + at)
        theirs = emb[pl.ds(y_at + at, step)]
        grad_emb[earlier] += dot_nn(weight[: rows + at], theirs)
        grad_emb[pl.ds(rows + at, step)] = dot_tn(weight, emb[pl.ds(own_at, rows + at + step)])
        turn(1, at, step)
        if j == 0:
            for i in range(2, tokens):
                heard(i - 1)
                pass_on(i)
            for k in range(4):
                part = pl.ds(k * quarter, quarter)
                flipped_map[:, part] = mapping[part].T
    finish(0)
    for copy in send_theirs:
        copy.wait_recv()
    weight = weights(diag_at, rows, y_at, rows, their_labels)
    grad_emb[pl.ds(rows, rows)] += dot_tn(weight, emb[pl.ds(diag_at, rows)])
    finish(1)

    def product(i, h):
        block = dot_nn(lhs[i], grad_pre[:, h * half : (h + 1) * half])
        block = block.reshape(nx, nz, 8, half)
        return jnp.concatenate([block[..., :quarter], block[..., quarter:]], axis=-2)

    sent = []

    def send(src, dst, sems, at, device):
        copy = remote(src, dst, sems, at, device)
        copy.start()
        sent.append(copy)
        return copy

    to_right, to_left = {"pair": right}, {"pair": left}
    core_copies, out_copies, z_copies, y_copies = [], [], [], []
    for h in range(2):
        core_out[h] = product(0, h).astype(BF16)
        core_copies.append(send(core_out.at[h], core_in.at[h], core_sem, h, to_core))
    for h in range(2):
        mine[h] = product(1, h)

    lo, hi = pl.ds(0, nz // 2), pl.ds(nz // 2, nz // 2)

    def send_x(h, i, src):
        return send(src, x_in.at[h, i], x_sem, 6 * h + i, to_left if i % 2 else to_right)

    def send_far(h):
        core_copies[h].wait_recv()
        total = mine[h] + core_in[h].astype(F32)
        mine[h] = total
        x_out[h] = total.astype(BF16)
        out_copies.append([send_x(h, 0, x_out.at[h, x_far, lo]), send_x(h, 1, x_out.at[h, x_far, hi])])

    def send_direct(h):
        out_copies[h].append(send_x(h, 2, x_out.at[h, x_right, hi]))
        out_copies[h].append(send_x(h, 3, x_out.at[h, x_left, lo]))

    def relay(h):
        for i, (x, part) in enumerate(((x_right, lo), (x_left, hi))):
            out_copies[h][i].wait_recv()
            relay_out[h, i] = (mine[h, x, part] + x_in[h, i].astype(F32)).astype(BF16)
            out_copies[h].append(send_x(h, 4 + i, relay_out.at[h, i]))

    send_far(0)
    send_far(1)
    send_direct(0)
    relay(0)
    send_direct(1)
    relay(1)
    if tokens > 0:
        heard(tokens - 1)
    pl.semaphore_wait(y_token, 1)
    for h in range(2):
        for copy in out_copies[h][2:]:
            copy.wait_recv()
        got = [x_in[h, i].astype(F32) for i in range(2, 6)]
        z_sum[h, lo] = mine[h, x_at, lo] + got[1] + got[2]
        z_sum[h, hi] = mine[h, x_at, hi] + got[0] + got[3]
        z_out[h] = z_sum[h].astype(BF16)
        z_copies.append(
            [
                send(
                    z_out.at[h, (z_at + d) % nz],
                    z_in.at[h, d - 1],
                    z_sem,
                    h * (nz - 1) + d - 1,
                    {"pair": z_mates[d - 1]},
                )
                for d in range(1, nz)
            ]
        )

    for h in range(2):
        total = z_sum[h, z_at]
        for d in range(1, nz):
            z_copies[h][d - 1].wait_recv()
            total = total + z_in[h, d - 1].astype(F32)
        y_in[h, group] = total.astype(BF16)
        y_copies.append(
            [
                send(
                    y_in.at[h, group],
                    y_in.at[h, group],
                    y_sem,
                    h * (groups - 1) + d - 1,
                    {"dp": y_groups[d - 1]},
                )
                for d in range(1, groups)
            ]
        )

    gf_vmem[...] = dot_nn(grad_pre[pl.ds(0, rows)], flipped_map[...]).astype(BF16)
    store_gf = pltpu.make_async_copy(gf_vmem, gf_hbm, local_sem.at[3])
    store_gf.start()

    for h in range(2):
        for copy in y_copies[h]:
            copy.wait_recv()
        total = y_in[h, 0].astype(F32)
        for at in range(1, groups):
            total = total + y_in[h, at].astype(F32)
        gp_ref[:, h * half : (h + 1) * half] = jnp.concatenate([total[:8], total[8:]], axis=-1)

    store_gf.wait()
    for copy in send_feat + [send_lab, send_own] + send_theirs + sent:
        copy.wait_send()


def body(nz, nx, groups, feats, mapping, sharp, offset, segments, targets):
    rows, width = feats.shape
    half, quarter = width // 2, width // 4
    smem = pl.BlockSpec(memory_space=pltpu.SMEM)
    anywhere = pl.BlockSpec(memory_space=pl.ANY)

    integers = jnp.concatenate([segments.reshape(1, -1), targets.reshape(1, -1)], axis=1)

    def sems(n):
        return pltpu.SemaphoreType.DMA((2, n))

    return pl.pallas_call(
        functools.partial(kernel, nz, nx, groups),
        out_shape=(
            jax.ShapeDtypeStruct((rows, width), BF16),
            jax.ShapeDtypeStruct((8, width), F32),
        ),
        in_specs=[smem, smem] + [anywhere] * 3,
        out_specs=(anywhere, pl.BlockSpec(memory_space=pltpu.VMEM)),
        scratch_shapes=[
            pltpu.SMEM((1,) + segments.shape, jnp.int32),
            pltpu.VMEM((2, rows, width), BF16),
            pltpu.VMEM((2, 1, rows), jnp.int32),
            pltpu.VMEM((width, width), BF16),
            pltpu.VMEM((width, width), BF16),
            pltpu.VMEM((2, rows, width), F32),
            pltpu.VMEM((2, rows, 1), F32),
            pltpu.VMEM((4 * rows, width), BF16),
            pltpu.VMEM((2 * rows, width), F32),
            pltpu.VMEM((2 * rows, width), BF16),
            pltpu.VMEM((nz, nx, 2, 2, 8, 2 * rows), F32),
            pltpu.VMEM((2, nx * nz * 8, 2 * rows), BF16),
            pltpu.VMEM((2, nx, nz, 16, quarter), F32),
            pltpu.VMEM((2, nx, nz, 16, quarter), BF16),
            pltpu.VMEM((2, nx, nz, 16, quarter), BF16),
            pltpu.VMEM((2, nx, nz, 16, quarter), BF16),
            pltpu.VMEM((2, 6, nz // 2, 16, quarter), BF16),
            pltpu.VMEM((2, 2, nz // 2, 16, quarter), BF16),
            pltpu.VMEM((2, nz, 16, quarter), F32),
            pltpu.VMEM((2, nz, 16, quarter), BF16),
            pltpu.VMEM((2, nz - 1, 16, quarter), BF16),
            pltpu.VMEM((2, groups, 16, quarter), BF16),
            pltpu.VMEM((rows, width), BF16),
            pltpu.SemaphoreType.DMA((5,)),
            sems(CHUNKS + 1),
            sems(CHUNKS + 1),
            sems(2),
            sems(12),
            sems(2 * (nz - 1)),
            sems(2 * (groups - 1)),
            pltpu.SemaphoreType.REGULAR((3, 2)),
            pltpu.SemaphoreType.REGULAR,
        ],
        compiler_params=pltpu.CompilerParams(
            collective_id=0, has_side_effects=True, vmem_limit_bytes=53 * 1024 * 1024
        ),
        cost_estimate=pl.CostEstimate(
            flops=2 * rows * width * (5 * width + 11 * rows),
            bytes_accessed=8 * rows * width,
            transcendentals=5 * rows * rows,
        ),
        name="contrastive",
    )(sharp, offset, integers, feats, mapping)


def solution(mesh, nx=NX):
    nz = mesh.shape["pair"] // (4 * nx)
    in_specs = (P(("pair", "dp"), None), P(), P(), P(), P(), P(("pair", "dp")))
    out_specs = (P(("pair", "dp"), None), P("pair", None))
    return jax.shard_map(
        functools.partial(body, nz, nx, mesh.shape["dp"]),
        mesh=mesh,
        in_specs=in_specs,
        out_specs=out_specs,
        check_vma=False,
    )
```

```python
import functools

import jax
import jax.numpy as jnp
from jax import lax
from jax.experimental import pallas as pl
from jax.experimental.pallas import tpu as pltpu
from jax.sharding import PartitionSpec as P

EPSILON = 1e-06
NX = 4
CHUNKS = 2
PIECES = 2
F32 = jnp.float32
BF16 = jnp.bfloat16


def dot_nn(a, b):
    return jnp.dot(a, b, preferred_element_type=F32)


def dot_nt(a, b):
    return lax.dot_general(a, b, (((1,), (1,)), ((), ())), preferred_element_type=F32)


def dot_tn(a, b):
    return lax.dot_general(a, b, (((0,), (0,)), ((), ())), preferred_element_type=F32)


def kernel(
    nz,
    nx,
    groups,
    sharp_ref,
    offset_ref,
    int_hbm,
    feat_hbm,
    map_hbm,
    gf_hbm,
    gp_ref,
    seg_ref,
    feats,
    labels,
    mapping,
    flipped_map,
    proj,
    inv,
    emb,
    grad_emb,
    grad_pre,
    turned,
    lhs,
    mine,
    core_out,
    core_in,
    x_out,
    x_in,
    relay_out,
    z_sum,
    z_out,
    z_in,
    y_in,
    gf_vmem,
    local_sem,
    feat_sem,
    emb_sem,
    core_sem,
    x_sem,
    z_sem,
    y_sem,
    z_token,
    y_token,
):
    rows, width = feat_hbm.shape
    half, quarter = width // 2, width // 4
    spans = [(0, rows - rows // 4), (rows - rows // 4, rows // 4)]
    blocks = seg_ref.shape[1]
    pair = lax.axis_index("pair")
    group = lax.axis_index("dp")
    core = pair % 2
    y_lo = (pair // 2) % 2
    x_at = (pair // 4) % nx
    z_at = pair // (4 * nx)
    core_mate = pair + 1 - 2 * core
    y_mate = pair + 2 - 4 * y_lo
    diag_mate = y_mate + 1 - 2 * core
    x_right, x_left, x_far = (x_at + 1) % nx, (x_at + nx - 1) % nx, (x_at + 2) % nx
    right, left = pair + (x_right - x_at) * 4, pair + (x_left - x_at) * 4
    z_mates = [pair + ((z_at + d) % nz - z_at) * (4 * nx) for d in range(1, nz)]
    y_groups = [(group + d) % groups for d in range(1, groups)]
    to_core, to_y = {"pair": core_mate}, {"pair": y_mate}

    load_feat = pltpu.make_async_copy(feat_hbm, feats.at[0], local_sem.at[0])
    load_map = pltpu.make_async_copy(map_hbm, mapping, local_sem.at[1])
    load_lab = pltpu.make_async_copy(int_hbm.at[:, pl.ds(blocks, rows)], labels.at[0], local_sem.at[2])
    load_seg = pltpu.make_async_copy(int_hbm.at[:, pl.ds(0, blocks)], seg_ref, local_sem.at[4])
    loads = [load_feat, load_map, load_lab, load_seg]
    for copy in loads:
        copy.start()

    def remote(src, dst, sems, at, device):
        return pltpu.make_async_remote_copy(
            src_ref=src,
            dst_ref=dst,
            send_sem=sems.at[0, at],
            recv_sem=sems.at[1, at],
            device_id=device,
            device_id_type=pl.DeviceIdType.MESH,
        )

    barrier = pltpu.get_barrier_semaphore()
    z_near = [{"pair": z_mates[0]}, {"pair": z_mates[-1]}]
    greeted = [to_core, to_y, {"pair": right}, {"pair": left}] + z_near
    greeted += [{"dp": y_groups[0]}, {"dp": y_groups[-1]}]
    for device in greeted:
        pl.semaphore_signal(barrier, inc=1, device_id=device, device_id_type=pl.DeviceIdType.MESH)
    pl.semaphore_wait(barrier, len(greeted))

    def pass_on(i):
        for side in range(2):
            pl.semaphore_signal(
                z_token.at[i, side],
                inc=1,
                device_id=z_near[side],
                device_id_type=pl.DeviceIdType.MESH,
            )

    def heard(i):
        for side in range(2):
            pl.semaphore_wait(z_token.at[i, side], 1)

    tokens = nz // 2 - 1
    if tokens > 0:
        pass_on(0)
    pl.semaphore_signal(
        y_token, inc=1, device_id={"dp": y_groups[0]}, device_id_type=pl.DeviceIdType.MESH
    )

    send_lab = remote(int_hbm.at[:, pl.ds(blocks, rows)], labels.at[1], feat_sem, CHUNKS, to_y)
    send_lab.start()

    send_feat = []
    for j, source in enumerate((feat_hbm, feats.at[0])):
        if j > 0:
            load_feat.wait()
        part = pl.ds(*spans[j])
        send_feat.append(remote(source.at[part], feats.at[1, part], feat_sem, j, to_y))
        send_feat[-1].start()

    mate_at, own_at, y_at, diag_at = 0, rows, 2 * rows, 3 * rows

    def embed(slot, start, size):
        part = pl.ds(start, size)
        projected = dot_nn(feats[slot, part], mapping[...])
        norm = lax.rsqrt(jnp.sum(projected * projected, axis=-1, keepdims=True) + EPSILON)
        proj[slot, part] = projected
        inv[slot, part] = norm
        emb[pl.ds((slot + 1) * rows + start, size)] = (projected * norm).astype(BF16)

    def turn(slot, start, size):
        flipped = feats[slot, pl.ds(start, size)].astype(F32).T
        at = pl.ds(slot * rows + start, size)
        turned[:, :, :, :, :, at] = flipped.reshape(turned.shape[:5] + (size,))
        for i, owner in enumerate((1 - core, core)):
            for x in range(nx):
                block = turned[:, x, y_lo, owner, :, at].reshape(nz * 8, size)
                lhs[i, pl.ds(x * nz * 8, nz * 8), at] = block.astype(BF16)

    def weights(left_at, left_size, right_at, right_size, right_labels):
        left = emb[pl.ds(left_at, left_size)]
        right = emb[pl.ds(right_at, right_size)]
        logits = dot_nt(left, right) * sharp + offset
        row = lax.broadcasted_iota(jnp.int32, logits.shape, 0) + left_at
        group_row = row + firsts[left_at // rows]
        for at in range(left_at // rows + 1, (left_at + left_size - 1) // rows + 1):
            group_row = jnp.where(row < at * rows, group_row, row + firsts[at])
        hit = jnp.where(right_labels == group_row, 1.0, 0.0)
        weight = (2.0 / groups * sharp) * (jax.nn.sigmoid(logits) - hit)
        if left_at < right_at + right_size and right_at < left_at + left_size:
            column = lax.broadcasted_iota(jnp.int32, logits.shape, 1) + right_at
            weight = jnp.where(row == column, 0.0, weight)
        return weight.astype(BF16)

    def finish(slot):
        part = pl.ds(slot * rows, rows)
        grad = grad_emb[part]
        projected = proj[slot]
        norm = inv[slot]
        inner = jnp.sum(projected * grad, axis=-1, keepdims=True)
        grad_pre[part] = (norm * grad - norm**3 * inner * projected).astype(BF16)

    load_map.wait()
    embed(0, 0, rows)
    send_own = remote(emb.at[pl.ds(own_at, rows)], emb.at[pl.ds(mate_at, rows)], emb_sem, 0, to_core)
    send_own.start()
    load_seg.wait()
    load_lab.wait()
    sharp = sharp_ref[0]
    offset = offset_ref[0]
    held = (core_mate, pair, y_mate, diag_mate)
    firsts = [(seg_ref[0, at] - i) * rows for i, at in enumerate(held)]
    own_labels = labels[0]
    turn(0, 0, rows)
    if tokens > 1:
        heard(0)
        pass_on(1)
    send_own.wait_recv()
    weight = weights(mate_at, 2 * rows, own_at, rows, own_labels)
    grad_emb[pl.ds(0, rows)] = dot_tn(weight, emb[pl.ds(mate_at, 2 * rows)])

    def forward(j):
        copy = remote(
            emb.at[pl.ds(y_at + spans[j][0], spans[j][1])],
            emb.at[pl.ds(diag_at + spans[j][0], spans[j][1])],
            emb_sem,
            1 + j,
            to_core,
        )
        copy.start()
        return copy

    send_lab.wait_recv()
    their_labels = labels[1]
    all_labels = jnp.concatenate([own_labels, their_labels], axis=1)
    send_theirs = []
    for j, (at, size) in enumerate(spans):
        send_feat[j].wait_recv()
        embed(1, at, size)
        send_theirs.append(forward(j))
        width_now = rows + at + size
        weight = weights(y_at + at, size, own_at, width_now, all_labels[:, :width_now])
        earlier = pl.ds(0, rows + at)
        theirs = emb[pl.ds(y_at + at, size)]
        grad_emb[pl.ds(rows + at, size)] = dot_nn(weight, emb[pl.ds(own_at, width_now)])
        grad_emb[earlier] += dot_tn(weight[:, : rows + at], theirs)
        turn(1, j * (rows // 2), rows // 2)
        if j == 0:
            for i in range(2, tokens):
                heard(i - 1)
                pass_on(i)
            for k in range(4):
                part = pl.ds(k * quarter, quarter)
                flipped_map[:, part] = mapping[part].T
    finish(0)
    for copy in send_theirs:
        copy.wait_recv()
    weight = weights(diag_at, rows, y_at, rows, their_labels)
    grad_emb[pl.ds(rows, rows)] += dot_tn(weight, emb[pl.ds(diag_at, rows)])
    finish(1)

    def product(i, h):
        block = dot_nn(lhs[i], grad_pre[:, h * half : (h + 1) * half])
        block = block.reshape(nx, nz, 8, half)
        return jnp.concatenate([block[..., :quarter], block[..., quarter:]], axis=-2)

    sent = []

    def send(src, dst, sems, at, device):
        copy = remote(src, dst, sems, at, device)
        copy.start()
        sent.append(copy)
        return copy

    to_right, to_left = {"pair": right}, {"pair": left}
    core_copies, out_copies, z_copies, y_copies = [], [], [], []
    for h in range(2):
        core_out[h] = product(0, h).astype(BF16)
        core_copies.append(send(core_out.at[h], core_in.at[h], core_sem, h, to_core))
    for h in range(2):
        mine[h] = product(1, h)

    lo, hi = pl.ds(0, nz // 2), pl.ds(nz // 2, nz // 2)

    def send_x(h, i, src):
        return send(src, x_in.at[h, i], x_sem, 6 * h + i, to_left if i % 2 else to_right)

    def send_far(h):
        core_copies[h].wait_recv()
        total = mine[h, x_far] + core_in[h, x_far].astype(F32)
        x_out[h, x_far] = total.astype(BF16)
        out_copies.append([send_x(h, 0, x_out.at[h, x_far, lo]), send_x(h, 1, x_out.at[h, x_far, hi])])
        for x in (x_right, x_left, x_at):
            total = mine[h, x] + core_in[h, x].astype(F32)
            mine[h, x] = total
            x_out[h, x] = total.astype(BF16)

    def send_direct(h):
        out_copies[h].append(send_x(h, 2, x_out.at[h, x_right, hi]))
        out_copies[h].append(send_x(h, 3, x_out.at[h, x_left, lo]))

    def relay(h):
        for i, (x, part) in enumerate(((x_right, lo), (x_left, hi))):
            out_copies[h][i].wait_recv()
            relay_out[h, i] = (mine[h, x, part] + x_in[h, i].astype(F32)).astype(BF16)
            out_copies[h].append(send_x(h, 4 + i, relay_out.at[h, i]))

    send_far(0)
    send_far(1)
    send_direct(0)
    relay(0)
    send_direct(1)
    relay(1)
    if tokens > 0:
        heard(tokens - 1)
    pl.semaphore_wait(y_token, 1)
    for h in range(2):
        for copy in out_copies[h][2:]:
            copy.wait_recv()
        got = [x_in[h, i].astype(F32) for i in range(2, 6)]
        z_sum[h, lo] = mine[h, x_at, lo] + got[1] + got[2]
        z_sum[h, hi] = mine[h, x_at, hi] + got[0] + got[3]
        z_out[h] = z_sum[h].astype(BF16)
        z_copies.append(
            [
                send(
                    z_out.at[h, (z_at + d) % nz],
                    z_in.at[h, d - 1],
                    z_sem,
                    h * (nz - 1) + d - 1,
                    {"pair": z_mates[d - 1]},
                )
                for d in range(1, nz)
            ]
        )

    for h in range(2):
        total = z_sum[h, z_at]
        for d in range(1, nz):
            z_copies[h][d - 1].wait_recv()
            total = total + z_in[h, d - 1].astype(F32)
        y_in[h, group] = total.astype(BF16)
        y_copies.append(
            [
                send(
                    y_in.at[h, group],
                    y_in.at[h, group],
                    y_sem,
                    h * (groups - 1) + d - 1,
                    {"dp": y_groups[d - 1]},
                )
                for d in range(1, groups)
            ]
        )

    gf_vmem[...] = dot_nn(grad_pre[pl.ds(0, rows)], flipped_map[...]).astype(BF16)
    store_gf = pltpu.make_async_copy(gf_vmem, gf_hbm, local_sem.at[3])
    store_gf.start()

    for h in range(2):
        for copy in y_copies[h]:
            copy.wait_recv()
        total = y_in[h, 0].astype(F32)
        for at in range(1, groups):
            total = total + y_in[h, at].astype(F32)
        gp_ref[:, h * half : (h + 1) * half] = jnp.concatenate([total[:8], total[8:]], axis=-1)

    store_gf.wait()
    for copy in send_feat + [send_lab, send_own] + send_theirs + sent:
        copy.wait_send()


def hand_over(gf_in, gp_in, gf_out, gp_out, sem):
    size = gf_in.shape[0] // PIECES
    copies = [pltpu.make_async_copy(gp_in, gp_out, sem.at[PIECES])]
    for i in range(PIECES):
        part = pl.ds(i * size, size)
        copies.append(pltpu.make_async_copy(gf_in.at[part], gf_out.at[part], sem.at[i]))
    for copy in copies:
        copy.start()
    for copy in copies:
        copy.wait()


def body(nz, nx, groups, feats, mapping, sharp, offset, segments, targets):
    rows, width = feats.shape
    half, quarter = width // 2, width // 4
    smem = pl.BlockSpec(memory_space=pltpu.SMEM)
    anywhere = pl.BlockSpec(memory_space=pl.ANY)

    integers = jnp.concatenate([segments.reshape(1, -1), targets.reshape(1, -1)], axis=1)

    def sems(n):
        return pltpu.SemaphoreType.DMA((2, n))

    results = pl.pallas_call(
        functools.partial(kernel, nz, nx, groups),
        out_shape=(
            jax.ShapeDtypeStruct((rows, width), BF16),
            jax.ShapeDtypeStruct((8, width), F32),
        ),
        in_specs=[smem, smem] + [anywhere] * 3,
        out_specs=(anywhere, pl.BlockSpec(memory_space=pltpu.VMEM)),
        scratch_shapes=[
            pltpu.SMEM((1,) + segments.shape, jnp.int32),
            pltpu.VMEM((2, rows, width), BF16),
            pltpu.VMEM((2, 1, rows), jnp.int32),
            pltpu.VMEM((width, width), BF16),
            pltpu.VMEM((width, width), BF16),
            pltpu.VMEM((2, rows, width), F32),
            pltpu.VMEM((2, rows, 1), F32),
            pltpu.VMEM((4 * rows, width), BF16),
            pltpu.VMEM((2 * rows, width), F32),
            pltpu.VMEM((2 * rows, width), BF16),
            pltpu.VMEM((nz, nx, 2, 2, 8, 2 * rows), F32),
            pltpu.VMEM((2, nx * nz * 8, 2 * rows), BF16),
            pltpu.VMEM((2, nx, nz, 16, quarter), F32),
            pltpu.VMEM((2, nx, nz, 16, quarter), BF16),
            pltpu.VMEM((2, nx, nz, 16, quarter), BF16),
            pltpu.VMEM((2, nx, nz, 16, quarter), BF16),
            pltpu.VMEM((2, 6, nz // 2, 16, quarter), BF16),
            pltpu.VMEM((2, 2, nz // 2, 16, quarter), BF16),
            pltpu.VMEM((2, nz, 16, quarter), F32),
            pltpu.VMEM((2, nz, 16, quarter), BF16),
            pltpu.VMEM((2, nz - 1, 16, quarter), BF16),
            pltpu.VMEM((2, groups, 16, quarter), BF16),
            pltpu.VMEM((rows, width), BF16),
            pltpu.SemaphoreType.DMA((5,)),
            sems(CHUNKS + 1),
            sems(CHUNKS + 1),
            sems(2),
            sems(12),
            sems(2 * (nz - 1)),
            sems(2 * (groups - 1)),
            pltpu.SemaphoreType.REGULAR((3, 2)),
            pltpu.SemaphoreType.REGULAR,
        ],
        compiler_params=pltpu.CompilerParams(
            collective_id=0, has_side_effects=True, vmem_limit_bytes=53 * 1024 * 1024
        ),
        cost_estimate=pl.CostEstimate(
            flops=2 * rows * width * (5 * width + 11 * rows),
            bytes_accessed=8 * rows * width,
            transcendentals=5 * rows * rows,
        ),
        name="contrastive",
    )(sharp, offset, integers, feats, mapping)
    return pl.pallas_call(
        hand_over,
        out_shape=(
            jax.ShapeDtypeStruct((rows, width), BF16),
            jax.ShapeDtypeStruct((8, width), F32),
        ),
        in_specs=[pl.BlockSpec(memory_space=pltpu.VMEM)] * 2,
        out_specs=(anywhere, anywhere),
        scratch_shapes=[pltpu.SemaphoreType.DMA((PIECES + 1,))],
        name="hand_over",
    )(*results)


def solution(mesh, nx=NX):
    nz = mesh.shape["pair"] // (4 * nx)
    in_specs = (P(("pair", "dp"), None), P(), P(), P(), P(), P(("pair", "dp")))
    out_specs = (P(("pair", "dp"), None), P("pair", None))
    return jax.shard_map(
        functools.partial(body, nz, nx, mesh.shape["dp"]),
        mesh=mesh,
        in_specs=in_specs,
        out_specs=out_specs,
        check_vma=False,
    )
```

```python
import functools

import jax
import jax.numpy as jnp
from jax import lax
from jax.experimental import pallas as pl
from jax.experimental.pallas import tpu as pltpu
from jax.sharding import PartitionSpec as P

EPSILON = 1e-06
NX = 4
CHUNKS = 2
PIECES = 2
F32 = jnp.float32
BF16 = jnp.bfloat16


def dot_nn(a, b):
    return jnp.dot(a, b, preferred_element_type=F32)


def dot_nt(a, b):
    return lax.dot_general(a, b, (((1,), (1,)), ((), ())), preferred_element_type=F32)


def dot_tn(a, b):
    return lax.dot_general(a, b, (((0,), (0,)), ((), ())), preferred_element_type=F32)


def kernel(
    nz,
    nx,
    groups,
    sharp_ref,
    offset_ref,
    int_hbm,
    feat_hbm,
    map_hbm,
    gf_hbm,
    gp_ref,
    seg_ref,
    feats,
    labels,
    mapping,
    flipped_map,
    proj,
    inv,
    emb,
    grad_emb,
    grad_pre,
    turned,
    lhs,
    mine,
    core_out,
    core_in,
    x_out,
    far_in,
    x_in,
    z_sum,
    z_out,
    z_in,
    y_in,
    gf_vmem,
    local_sem,
    feat_sem,
    emb_sem,
    core_sem,
    x_sem,
    z_sem,
    y_sem,
    z_token,
    y_token,
):
    rows, width = feat_hbm.shape
    half = width // PIECES
    quarter = half // 2
    step = rows // CHUNKS
    blocks = seg_ref.shape[1]
    pair = lax.axis_index("pair")
    group = lax.axis_index("dp")
    core = pair % 2
    y_lo = (pair // 2) % 2
    x_at = (pair // 4) % nx
    z_at = pair // (4 * nx)
    core_mate = pair + 1 - 2 * core
    y_mate = pair + 2 - 4 * y_lo
    diag_mate = y_mate + 1 - 2 * core
    x_right, x_left, x_far = (x_at + 1) % nx, (x_at + nx - 1) % nx, (x_at + 2) % nx
    right, left = pair + (x_right - x_at) * 4, pair + (x_left - x_at) * 4
    z_mates = [pair + ((z_at + d) % nz - z_at) * (4 * nx) for d in range(1, nz)]
    y_groups = [(group + d) % groups for d in range(1, groups)]
    to_core, to_y = {"pair": core_mate}, {"pair": y_mate}

    load_feat = pltpu.make_async_copy(feat_hbm, feats.at[0], local_sem.at[0])
    load_map = pltpu.make_async_copy(map_hbm, mapping, local_sem.at[1])
    load_lab = pltpu.make_async_copy(int_hbm.at[:, pl.ds(blocks, rows)], labels.at[0], local_sem.at[2])
    load_seg = pltpu.make_async_copy(int_hbm.at[:, pl.ds(0, blocks)], seg_ref, local_sem.at[4])
    loads = [load_feat, load_map, load_lab, load_seg]
    for copy in loads:
        copy.start()

    def remote(src, dst, sems, at, device):
        return pltpu.make_async_remote_copy(
            src_ref=src,
            dst_ref=dst,
            send_sem=sems.at[0, at],
            recv_sem=sems.at[1, at],
            device_id=device,
            device_id_type=pl.DeviceIdType.MESH,
        )

    barrier = pltpu.get_barrier_semaphore()
    z_near = [{"pair": z_mates[0]}, {"pair": z_mates[-1]}]
    greeted = [to_core, to_y, {"pair": right}, {"pair": left}] + z_near
    greeted += [{"dp": y_groups[0]}, {"dp": y_groups[-1]}]
    for device in greeted:
        pl.semaphore_signal(barrier, inc=1, device_id=device, device_id_type=pl.DeviceIdType.MESH)
    pl.semaphore_wait(barrier, len(greeted))

    def pass_on(i):
        for side in range(2):
            pl.semaphore_signal(
                z_token.at[i, side],
                inc=1,
                device_id=z_near[side],
                device_id_type=pl.DeviceIdType.MESH,
            )

    def heard(i):
        for side in range(2):
            pl.semaphore_wait(z_token.at[i, side], 1)

    tokens = nz // 2 - 1
    if tokens > 0:
        pass_on(0)
    pl.semaphore_signal(
        y_token, inc=1, device_id={"dp": y_groups[0]}, device_id_type=pl.DeviceIdType.MESH
    )

    send_lab = remote(int_hbm.at[:, pl.ds(blocks, rows)], labels.at[1], feat_sem, CHUNKS, to_y)
    send_lab.start()

    send_feat = []
    for j, source in enumerate((feat_hbm, feats.at[0])):
        if j > 0:
            load_feat.wait()
        part = pl.ds(j * step, step)
        send_feat.append(remote(source.at[part], feats.at[1, part], feat_sem, j, to_y))
        send_feat[-1].start()

    mate_at, own_at, y_at, diag_at = 0, rows, 2 * rows, 3 * rows

    def embed(slot, start, size):
        part = pl.ds(start, size)
        projected = dot_nn(feats[slot, part], mapping[...])
        norm = lax.rsqrt(jnp.sum(projected * projected, axis=-1, keepdims=True) + EPSILON)
        proj[slot, part] = projected
        inv[slot, part] = norm
        emb[pl.ds((slot + 1) * rows + start, size)] = (projected * norm).astype(BF16)

    def turn(slot, start, size):
        flipped = feats[slot, pl.ds(start, size)].astype(F32).T
        at = pl.ds(slot * rows + start, size)
        turned[:, :, :, :, :, at] = flipped.reshape(turned.shape[:5] + (size,))
        for i, owner in enumerate((1 - core, core)):
            for x in range(nx):
                block = turned[:, x, y_lo, owner, :, at].reshape(nz * 8, size)
                lhs[i, pl.ds(x * nz * 8, nz * 8), at] = block.astype(BF16)

    def weights(left_at, left_size, right_at, right_size, right_labels):
        left = emb[pl.ds(left_at, left_size)]
        right = emb[pl.ds(right_at, right_size)]
        logits = dot_nt(left, right) * sharp + offset
        row = lax.broadcasted_iota(jnp.int32, logits.shape, 0) + left_at
        group_row = row + firsts[left_at // rows]
        for at in range(left_at // rows + 1, (left_at + left_size - 1) // rows + 1):
            group_row = jnp.where(row < at * rows, group_row, row + firsts[at])
        hit = jnp.where(right_labels == group_row, 1.0, 0.0)
        weight = (2.0 / groups * sharp) * (jax.nn.sigmoid(logits) - hit)
        if left_at < right_at + right_size and right_at < left_at + left_size:
            column = lax.broadcasted_iota(jnp.int32, logits.shape, 1) + right_at
            weight = jnp.where(row == column, 0.0, weight)
        return weight.astype(BF16)

    def finish(slot):
        part = pl.ds(slot * rows, rows)
        grad = grad_emb[part]
        projected = proj[slot]
        norm = inv[slot]
        inner = jnp.sum(projected * grad, axis=-1, keepdims=True)
        grad_pre[part] = (norm * grad - norm**3 * inner * projected).astype(BF16)

    load_map.wait()
    embed(0, 0, rows)
    send_own = remote(emb.at[pl.ds(own_at, rows)], emb.at[pl.ds(mate_at, rows)], emb_sem, 0, to_core)
    send_own.start()
    load_seg.wait()
    load_lab.wait()
    sharp = sharp_ref[0]
    offset = offset_ref[0]
    held = (core_mate, pair, y_mate, diag_mate)
    firsts = [(seg_ref[0, at] - i) * rows for i, at in enumerate(held)]
    own_labels = labels[0]
    turn(0, 0, rows)
    if tokens > 1:
        heard(0)
        pass_on(1)
    send_own.wait_recv()
    weight = weights(mate_at, 2 * rows, own_at, rows, own_labels)
    grad_emb[pl.ds(0, rows)] = dot_tn(weight, emb[pl.ds(mate_at, 2 * rows)])

    def forward(j):
        copy = remote(
            emb.at[pl.ds(y_at + j * step, step)],
            emb.at[pl.ds(diag_at + j * step, step)],
            emb_sem,
            1 + j,
            to_core,
        )
        copy.start()
        return copy

    send_lab.wait_recv()
    their_labels = labels[1]
    send_theirs = []
    for j in range(CHUNKS):
        at = j * step
        send_feat[j].wait_recv()
        embed(1, at, step)
        send_theirs.append(forward(j))
        weight = weights(
            own_at, rows + at + step, y_at + at, step, their_labels[:, at : at + step]
        )
        earlier = pl.ds(0, rows + at)
        theirs = emb[pl.ds(y_at + at, step)]
        grad_emb[earlier] += dot_nn(weight[: rows + at], theirs)
        grad_emb[pl.ds(rows + at, step)] = dot_tn(weight, emb[pl.ds(own_at, rows + at + step)])
        turn(1, at, step)
        if j == 0:
            for i in range(2, tokens):
                heard(i - 1)
                pass_on(i)
            for k in range(4):
                part = pl.ds(k * (width // 4), width // 4)
                flipped_map[:, part] = mapping[part].T
    finish(0)
    for copy in send_theirs:
        copy.wait_recv()
    weight = weights(diag_at, rows, y_at, rows, their_labels)
    grad_emb[pl.ds(rows, rows)] += dot_tn(weight, emb[pl.ds(diag_at, rows)])
    finish(1)

    def product(i, h):
        block = dot_nn(lhs[i], grad_pre[:, h * half : (h + 1) * half])
        block = block.reshape(nx, nz, 8, half)
        return jnp.concatenate([block[..., :quarter], block[..., quarter:]], axis=-2)

    sent = []

    def send(src, dst, sems, at, device):
        copy = remote(src, dst, sems, at, device)
        copy.start()
        sent.append(copy)
        return copy

    to_right, to_left = {"pair": right}, {"pair": left}
    core_copies, out_copies, z_copies, y_copies = [], [], [], []
    for h in range(PIECES):
        core_out[h] = product(0, h).astype(BF16)
        core_copies.append(send(core_out.at[h], core_in.at[h], core_sem, h, to_core))
    for h in range(PIECES):
        mine[h] = product(1, h)

    lo, hi = pl.ds(0, nz // 2), pl.ds(nz // 2, nz // 2)

    def send_x(h, i, src, dst):
        return send(src, dst, x_sem, 4 * h + i, to_left if i % 2 else to_right)

    def send_far(h):
        core_copies[h].wait_recv()
        total = mine[h] + core_in[h].astype(F32)
        mine[h] = total
        x_out[h] = total.astype(BF16)
        out_copies.append(
            [
                send_x(h, i, x_out.at[h, x_far, part], far_in.at[h, i])
                for i, part in enumerate((lo, hi))
            ]
        )

    def relay(h):
        for i, (x, part) in enumerate(((x_right, lo), (x_left, hi))):
            out_copies[h][i].wait_recv()
            x_out[h, x, part] = (mine[h, x, part] + far_in[h, i].astype(F32)).astype(BF16)
            out_copies[h].append(send_x(h, 2 + i, x_out.at[h, x], x_in.at[h, i]))

    far_first = sorted(range(1, nz), key=lambda d: -min(d, nz - d))
    far_groups = sorted(range(1, groups), key=lambda d: -min(d, groups - d))

    def send_z(h):
        for copy in out_copies[h][2:]:
            copy.wait_recv()
        z_sum[h] = mine[h, x_at] + x_in[h, 0].astype(F32) + x_in[h, 1].astype(F32)
        z_out[h] = z_sum[h].astype(BF16)
        z_copies.append(
            [
                send(
                    z_out.at[h, (z_at + d) % nz],
                    z_in.at[h, d - 1],
                    z_sem,
                    h * (nz - 1) + d - 1,
                    {"pair": z_mates[d - 1]},
                )
                for d in far_first
            ]
        )

    def send_y(h):
        for copy in z_copies[h]:
            copy.wait_recv()
        total = z_sum[h, z_at]
        for d in range(1, nz):
            total = total + z_in[h, d - 1].astype(F32)
        y_in[h, group] = total.astype(BF16)
        y_copies.append(
            [
                send(
                    y_in.at[h, group],
                    y_in.at[h, group],
                    y_sem,
                    h * (groups - 1) + d - 1,
                    {"dp": y_groups[d - 1]},
                )
                for d in far_groups
            ]
        )

    send_far(0)
    for h in range(1, PIECES + 1):
        if h < PIECES:
            send_far(h)
        relay(h - 1)
        if h == 2:
            if tokens > 0:
                heard(tokens - 1)
            pl.semaphore_wait(y_token, 1)
        if h >= 2:
            send_z(h - 2)
    send_z(PIECES - 1)
    for h in range(PIECES):
        send_y(h)

    gf_vmem[...] = dot_nn(grad_pre[pl.ds(0, rows)], flipped_map[...]).astype(BF16)
    store_gf = pltpu.make_async_copy(gf_vmem, gf_hbm, local_sem.at[3])
    store_gf.start()

    for h in range(PIECES):
        for copy in y_copies[h]:
            copy.wait_recv()
        total = y_in[h, 0].astype(F32)
        for at in range(1, groups):
            total = total + y_in[h, at].astype(F32)
        gp_ref[:, h * half : (h + 1) * half] = jnp.concatenate([total[:8], total[8:]], axis=-1)

    store_gf.wait()
    for copy in send_feat + [send_lab, send_own] + send_theirs + sent:
        copy.wait_send()


def body(nz, nx, groups, feats, mapping, sharp, offset, segments, targets):
    rows, width = feats.shape
    half = width // PIECES
    quarter = half // 2
    smem = pl.BlockSpec(memory_space=pltpu.SMEM)
    anywhere = pl.BlockSpec(memory_space=pl.ANY)

    integers = jnp.concatenate([segments.reshape(1, -1), targets.reshape(1, -1)], axis=1)

    def sems(n):
        return pltpu.SemaphoreType.DMA((2, n))

    return pl.pallas_call(
        functools.partial(kernel, nz, nx, groups),
        out_shape=(
            jax.ShapeDtypeStruct((rows, width), BF16),
            jax.ShapeDtypeStruct((8, width), F32),
        ),
        in_specs=[smem, smem] + [anywhere] * 3,
        out_specs=(anywhere, pl.BlockSpec(memory_space=pltpu.VMEM)),
        scratch_shapes=[
            pltpu.SMEM((1,) + segments.shape, jnp.int32),
            pltpu.VMEM((2, rows, width), BF16),
            pltpu.VMEM((2, 1, rows), jnp.int32),
            pltpu.VMEM((width, width), BF16),
            pltpu.VMEM((width, width), BF16),
            pltpu.VMEM((2, rows, width), F32),
            pltpu.VMEM((2, rows, 1), F32),
            pltpu.VMEM((4 * rows, width), BF16),
            pltpu.VMEM((2 * rows, width), F32),
            pltpu.VMEM((2 * rows, width), BF16),
            pltpu.VMEM((nz, nx, 2, 2, 8, 2 * rows), F32),
            pltpu.VMEM((2, nx * nz * 8, 2 * rows), BF16),
            pltpu.VMEM((PIECES, nx, nz, 16, quarter), F32),
            pltpu.VMEM((PIECES, nx, nz, 16, quarter), BF16),
            pltpu.VMEM((PIECES, nx, nz, 16, quarter), BF16),
            pltpu.VMEM((PIECES, nx, nz, 16, quarter), BF16),
            pltpu.VMEM((PIECES, 2, nz // 2, 16, quarter), BF16),
            pltpu.VMEM((PIECES, 2, nz, 16, quarter), BF16),
            pltpu.VMEM((PIECES, nz, 16, quarter), F32),
            pltpu.VMEM((PIECES, nz, 16, quarter), BF16),
            pltpu.VMEM((PIECES, nz - 1, 16, quarter), BF16),
            pltpu.VMEM((PIECES, groups, 16, quarter), BF16),
            pltpu.VMEM((rows, width), BF16),
            pltpu.SemaphoreType.DMA((5,)),
            sems(CHUNKS + 1),
            sems(CHUNKS + 1),
            sems(PIECES),
            sems(4 * PIECES),
            sems(PIECES * (nz - 1)),
            sems(PIECES * (groups - 1)),
            pltpu.SemaphoreType.REGULAR((3, 2)),
            pltpu.SemaphoreType.REGULAR,
        ],
        compiler_params=pltpu.CompilerParams(
            collective_id=0, has_side_effects=True, vmem_limit_bytes=53 * 1024 * 1024
        ),
        cost_estimate=pl.CostEstimate(
            flops=2 * rows * width * (5 * width + 11 * rows),
            bytes_accessed=8 * rows * width,
            transcendentals=5 * rows * rows,
        ),
        name="contrastive",
    )(sharp, offset, integers, feats, mapping)


def solution(mesh, nx=NX):
    nz = mesh.shape["pair"] // (4 * nx)
    in_specs = (P(("pair", "dp"), None), P(), P(), P(), P(), P(("pair", "dp")))
    out_specs = (P(("pair", "dp"), None), P("pair", None))
    return jax.shard_map(
        functools.partial(body, nz, nx, mesh.shape["dp"]),
        mesh=mesh,
        in_specs=in_specs,
        out_specs=out_specs,
        check_vma=False,
    )
```

```python
import functools

import jax
import jax.numpy as jnp
from jax import lax
from jax.experimental import pallas as pl
from jax.experimental.pallas import tpu as pltpu
from jax.sharding import PartitionSpec as P

EPSILON = 1e-06
NX = 4
CHUNKS = 2
PIECES = 2
F32 = jnp.float32
BF16 = jnp.bfloat16


def dot_nn(a, b):
    return jnp.dot(a, b, preferred_element_type=F32)


def dot_nt(a, b):
    return lax.dot_general(a, b, (((1,), (1,)), ((), ())), preferred_element_type=F32)


def dot_tn(a, b):
    return lax.dot_general(a, b, (((0,), (0,)), ((), ())), preferred_element_type=F32)


def kernel(
    nz,
    nx,
    groups,
    sharp_ref,
    offset_ref,
    int_hbm,
    feat_hbm,
    map_hbm,
    gf_hbm,
    gp_ref,
    seg_ref,
    feats,
    labels,
    mapping,
    flipped_map,
    proj,
    inv,
    emb,
    grad_emb,
    grad_pre,
    turned,
    lhs,
    mine,
    core_out,
    core_in,
    x_out,
    far_in,
    x_in,
    z_sum,
    z_out,
    z_in,
    y_in,
    gf_vmem,
    local_sem,
    feat_sem,
    emb_sem,
    core_sem,
    x_sem,
    z_sem,
    y_sem,
    z_token,
    y_token,
):
    rows, width = feat_hbm.shape
    half = width // PIECES
    quarter = half // 2
    step = rows // CHUNKS
    blocks = seg_ref.shape[1]
    pair = lax.axis_index("pair")
    group = lax.axis_index("dp")
    core = pair % 2
    y_lo = (pair // 2) % 2
    x_at = (pair // 4) % nx
    z_at = pair // (4 * nx)
    core_mate = pair + 1 - 2 * core
    y_mate = pair + 2 - 4 * y_lo
    diag_mate = y_mate + 1 - 2 * core
    x_right, x_left, x_far = (x_at + 1) % nx, (x_at + nx - 1) % nx, (x_at + 2) % nx
    right, left = pair + (x_right - x_at) * 4, pair + (x_left - x_at) * 4
    z_mates = [pair + ((z_at + d) % nz - z_at) * (4 * nx) for d in range(1, nz)]
    y_groups = [(group + d) % groups for d in range(1, groups)]
    to_core, to_y = {"pair": core_mate}, {"pair": y_mate}

    load_feat = pltpu.make_async_copy(feat_hbm, feats.at[0], local_sem.at[0])
    load_map = pltpu.make_async_copy(map_hbm, mapping, local_sem.at[1])
    load_lab = pltpu.make_async_copy(int_hbm.at[:, pl.ds(blocks, rows)], labels.at[0], local_sem.at[2])
    load_seg = pltpu.make_async_copy(int_hbm.at[:, pl.ds(0, blocks)], seg_ref, local_sem.at[4])
    loads = [load_feat, load_map, load_lab, load_seg]
    for copy in loads:
        copy.start()

    def remote(src, dst, sems, at, device):
        return pltpu.make_async_remote_copy(
            src_ref=src,
            dst_ref=dst,
            send_sem=sems.at[0, at],
            recv_sem=sems.at[1, at],
            device_id=device,
            device_id_type=pl.DeviceIdType.MESH,
        )

    barrier = pltpu.get_barrier_semaphore()
    z_near = [{"pair": z_mates[0]}, {"pair": z_mates[-1]}]
    greeted = [to_core, to_y, {"pair": right}, {"pair": left}] + z_near
    greeted += [{"dp": y_groups[0]}, {"dp": y_groups[-1]}]
    for device in greeted:
        pl.semaphore_signal(barrier, inc=1, device_id=device, device_id_type=pl.DeviceIdType.MESH)
    pl.semaphore_wait(barrier, len(greeted))

    def pass_on(i):
        for side in range(2):
            pl.semaphore_signal(
                z_token.at[i, side],
                inc=1,
                device_id=z_near[side],
                device_id_type=pl.DeviceIdType.MESH,
            )

    def heard(i):
        for side in range(2):
            pl.semaphore_wait(z_token.at[i, side], 1)

    tokens = nz // 2 - 1
    if tokens > 0:
        pass_on(0)
    pl.semaphore_signal(
        y_token, inc=1, device_id={"dp": y_groups[0]}, device_id_type=pl.DeviceIdType.MESH
    )

    send_lab = remote(int_hbm.at[:, pl.ds(blocks, rows)], labels.at[1], feat_sem, CHUNKS, to_y)
    send_lab.start()

    send_feat = []
    for j, source in enumerate((feat_hbm, feats.at[0])):
        if j > 0:
            load_feat.wait()
        part = pl.ds(j * step, step)
        send_feat.append(remote(source.at[part], feats.at[1, part], feat_sem, j, to_y))
        send_feat[-1].start()

    mate_at, own_at, y_at, diag_at = 0, rows, 2 * rows, 3 * rows

    def embed(slot, start, size):
        part = pl.ds(start, size)
        projected = dot_nn(feats[slot, part], mapping[...])
        norm = lax.rsqrt(jnp.sum(projected * projected, axis=-1, keepdims=True) + EPSILON)
        proj[slot, part] = projected
        inv[slot, part] = norm
        emb[pl.ds((slot + 1) * rows + start, size)] = (projected * norm).astype(BF16)

    def turn(slot, start, size):
        flipped = feats[slot, pl.ds(start, size)].astype(F32).T
        at = pl.ds(slot * rows + start, size)
        turned[:, :, :, :, :, at] = flipped.reshape(turned.shape[:5] + (size,))
        for i, owner in enumerate((1 - core, core)):
            for x in range(nx):
                block = turned[:, x, y_lo, owner, :, at].reshape(nz * 8, size)
                lhs[i, pl.ds(x * nz * 8, nz * 8), at] = block.astype(BF16)

    def weights(left_at, left_size, right_at, right_size, right_labels):
        left = emb[pl.ds(left_at, left_size)]
        right = emb[pl.ds(right_at, right_size)]
        logits = dot_nt(left, right) * sharp + offset
        row = lax.broadcasted_iota(jnp.int32, logits.shape, 0) + left_at
        group_row = row + firsts[left_at // rows]
        for at in range(left_at // rows + 1, (left_at + left_size - 1) // rows + 1):
            group_row = jnp.where(row < at * rows, group_row, row + firsts[at])
        hit = jnp.where(right_labels == group_row, 1.0, 0.0)
        weight = (2.0 / groups * sharp) * (jax.nn.sigmoid(logits) - hit)
        if left_at < right_at + right_size and right_at < left_at + left_size:
            column = lax.broadcasted_iota(jnp.int32, logits.shape, 1) + right_at
            weight = jnp.where(row == column, 0.0, weight)
        return weight.astype(BF16)

    def finish(slot):
        part = pl.ds(slot * rows, rows)
        grad = grad_emb[part]
        projected = proj[slot]
        norm = inv[slot]
        inner = jnp.sum(projected * grad, axis=-1, keepdims=True)
        grad_pre[part] = (norm * grad - norm**3 * inner * projected).astype(BF16)

    load_map.wait()
    embed(0, 0, rows)
    send_own = remote(emb.at[pl.ds(own_at, rows)], emb.at[pl.ds(mate_at, rows)], emb_sem, 0, to_core)
    send_own.start()
    load_seg.wait()
    load_lab.wait()
    sharp = sharp_ref[0]
    offset = offset_ref[0]
    held = (core_mate, pair, y_mate, diag_mate)
    firsts = [(seg_ref[0, at] - i) * rows for i, at in enumerate(held)]
    own_labels = labels[0]
    turn(0, 0, rows)
    if tokens > 1:
        heard(0)
        pass_on(1)
    send_own.wait_recv()
    weight = weights(mate_at, 2 * rows, own_at, rows, own_labels)
    grad_emb[pl.ds(0, rows)] = dot_tn(weight, emb[pl.ds(mate_at, 2 * rows)])

    def forward(j):
        copy = remote(
            emb.at[pl.ds(y_at + j * step, step)],
            emb.at[pl.ds(diag_at + j * step, step)],
            emb_sem,
            1 + j,
            to_core,
        )
        copy.start()
        return copy

    send_lab.wait_recv()
    their_labels = labels[1]
    send_theirs = []
    for j in range(CHUNKS):
        at = j * step
        send_feat[j].wait_recv()
        embed(1, at, step)
        send_theirs.append(forward(j))
        weight = weights(
            own_at, rows + at + step, y_at + at, step, their_labels[:, at : at + step]
        )
        earlier = pl.ds(0, rows + at)
        theirs = emb[pl.ds(y_at + at, step)]
        grad_emb[earlier] += dot_nn(weight[: rows + at], theirs)
        grad_emb[pl.ds(rows + at, step)] = dot_tn(weight, emb[pl.ds(own_at, rows + at + step)])
        turn(1, at, step)
        if j == 0:
            for i in range(2, tokens):
                heard(i - 1)
                pass_on(i)
            for k in range(4):
                part = pl.ds(k * (width // 4), width // 4)
                flipped_map[:, part] = mapping[part].T
    finish(0)
    for copy in send_theirs:
        copy.wait_recv()
    weight = weights(diag_at, rows, y_at, rows, their_labels)
    grad_emb[pl.ds(rows, rows)] += dot_tn(weight, emb[pl.ds(diag_at, rows)])
    finish(1)

    def product(i, h):
        block = dot_nn(lhs[i], grad_pre[:, h * half : (h + 1) * half])
        block = block.reshape(nx, nz, 8, half)
        return jnp.concatenate([block[..., :quarter], block[..., quarter:]], axis=-2)

    sent = []

    def send(src, dst, sems, at, device):
        copy = remote(src, dst, sems, at, device)
        copy.start()
        sent.append(copy)
        return copy

    to_right, to_left = {"pair": right}, {"pair": left}
    core_copies, out_copies, z_copies, y_copies = [], [], [], []
    for h in range(PIECES):
        core_out[h] = product(0, h).astype(BF16)
        core_copies.append(send(core_out.at[h], core_in.at[h], core_sem, h, to_core))
    for h in range(PIECES):
        mine[h] = product(1, h)

    lo, hi = pl.ds(0, nz // 2), pl.ds(nz // 2, nz // 2)

    def send_x(h, i, src, dst):
        return send(src, dst, x_sem, 4 * h + i, to_left if i % 2 else to_right)

    def send_far(h):
        core_copies[h].wait_recv()
        total = mine[h] + core_in[h].astype(F32)
        mine[h] = total
        x_out[h] = total.astype(BF16)
        out_copies.append(
            [
                send_x(h, i, x_out.at[h, x_far, part], far_in.at[h, i])
                for i, part in enumerate((lo, hi))
            ]
        )

    def relay(h):
        for i, (x, part) in enumerate(((x_right, lo), (x_left, hi))):
            out_copies[h][i].wait_recv()
            x_out[h, x, part] = (mine[h, x, part] + far_in[h, i].astype(F32)).astype(BF16)
            out_copies[h].append(send_x(h, 2 + i, x_out.at[h, x], x_in.at[h, i]))

    far_first = sorted(range(1, nz), key=lambda d: -min(d, nz - d))
    far_groups = sorted(range(1, groups), key=lambda d: -min(d, groups - d))

    def sum_x(h):
        for copy in out_copies[h][2:]:
            copy.wait_recv()
        total = mine[h, x_at] + x_in[h, 0].astype(F32) + x_in[h, 1].astype(F32)
        z_sum[:, h] = total
        z_out[:, h] = total.astype(BF16)

    send_far(0)
    for h in range(1, PIECES + 1):
        if h < PIECES:
            send_far(h)
        relay(h - 1)
    for h in range(PIECES):
        sum_x(h)
    if tokens > 0:
        heard(tokens - 1)
    pl.semaphore_wait(y_token, 1)
    for d in far_first:
        to_mate = {"pair": z_mates[d - 1]}
        z_copies.append(send(z_out.at[(z_at + d) % nz], z_in.at[d - 1], z_sem, d - 1, to_mate))
    for copy in z_copies:
        copy.wait_recv()
    total = z_sum[z_at]
    for d in range(1, nz):
        total = total + z_in[d - 1].astype(F32)
    y_in[group] = total.astype(BF16)
    for d in far_groups:
        to_group = {"dp": y_groups[d - 1]}
        y_copies.append(send(y_in.at[group], y_in.at[group], y_sem, d - 1, to_group))

    gf_vmem[...] = dot_nn(grad_pre[pl.ds(0, rows)], flipped_map[...]).astype(BF16)
    store_gf = pltpu.make_async_copy(gf_vmem, gf_hbm, local_sem.at[3])
    store_gf.start()

    for copy in y_copies:
        copy.wait_recv()
    total = y_in[0].astype(F32)
    for at in range(1, groups):
        total = total + y_in[at].astype(F32)
    for h in range(PIECES):
        gp_ref[:, h * half : (h + 1) * half] = jnp.concatenate(
            [total[h, :8], total[h, 8:]], axis=-1
        )

    store_gf.wait()
    for copy in send_feat + [send_lab, send_own] + send_theirs + sent:
        copy.wait_send()


def body(nz, nx, groups, feats, mapping, sharp, offset, segments, targets):
    rows, width = feats.shape
    half = width // PIECES
    quarter = half // 2
    smem = pl.BlockSpec(memory_space=pltpu.SMEM)
    anywhere = pl.BlockSpec(memory_space=pl.ANY)

    integers = jnp.concatenate([segments.reshape(1, -1), targets.reshape(1, -1)], axis=1)

    def sems(n):
        return pltpu.SemaphoreType.DMA((2, n))

    return pl.pallas_call(
        functools.partial(kernel, nz, nx, groups),
        out_shape=(
            jax.ShapeDtypeStruct((rows, width), BF16),
            jax.ShapeDtypeStruct((8, width), F32),
        ),
        in_specs=[smem, smem] + [anywhere] * 3,
        out_specs=(anywhere, pl.BlockSpec(memory_space=pltpu.VMEM)),
        scratch_shapes=[
            pltpu.SMEM((1,) + segments.shape, jnp.int32),
            pltpu.VMEM((2, rows, width), BF16),
            pltpu.VMEM((2, 1, rows), jnp.int32),
            pltpu.VMEM((width, width), BF16),
            pltpu.VMEM((width, width), BF16),
            pltpu.VMEM((2, rows, width), F32),
            pltpu.VMEM((2, rows, 1), F32),
            pltpu.VMEM((4 * rows, width), BF16),
            pltpu.VMEM((2 * rows, width), F32),
            pltpu.VMEM((2 * rows, width), BF16),
            pltpu.VMEM((nz, nx, 2, 2, 8, 2 * rows), F32),
            pltpu.VMEM((2, nx * nz * 8, 2 * rows), BF16),
            pltpu.VMEM((PIECES, nx, nz, 16, quarter), F32),
            pltpu.VMEM((PIECES, nx, nz, 16, quarter), BF16),
            pltpu.VMEM((PIECES, nx, nz, 16, quarter), BF16),
            pltpu.VMEM((PIECES, nx, nz, 16, quarter), BF16),
            pltpu.VMEM((PIECES, 2, nz // 2, 16, quarter), BF16),
            pltpu.VMEM((PIECES, 2, nz, 16, quarter), BF16),
            pltpu.VMEM((nz, PIECES, 16, quarter), F32),
            pltpu.VMEM((nz, PIECES, 16, quarter), BF16),
            pltpu.VMEM((nz - 1, PIECES, 16, quarter), BF16),
            pltpu.VMEM((groups, PIECES, 16, quarter), BF16),
            pltpu.VMEM((rows, width), BF16),
            pltpu.SemaphoreType.DMA((5,)),
            sems(CHUNKS + 1),
            sems(CHUNKS + 1),
            sems(PIECES),
            sems(4 * PIECES),
            sems(nz - 1),
            sems(groups - 1),
            pltpu.SemaphoreType.REGULAR((3, 2)),
            pltpu.SemaphoreType.REGULAR,
        ],
        compiler_params=pltpu.CompilerParams(
            collective_id=0, has_side_effects=True, vmem_limit_bytes=53 * 1024 * 1024
        ),
        cost_estimate=pl.CostEstimate(
            flops=2 * rows * width * (5 * width + 11 * rows),
            bytes_accessed=8 * rows * width,
            transcendentals=5 * rows * rows,
        ),
        name="contrastive",
    )(sharp, offset, integers, feats, mapping)


def solution(mesh, nx=NX):
    nz = mesh.shape["pair"] // (4 * nx)
    in_specs = (P(("pair", "dp"), None), P(), P(), P(), P(), P(("pair", "dp")))
    out_specs = (P(("pair", "dp"), None), P("pair", None))
    return jax.shard_map(
        functools.partial(body, nz, nx, mesh.shape["dp"]),
        mesh=mesh,
        in_specs=in_specs,
        out_specs=out_specs,
        check_vma=False,
    )
```
